32 devices in a mesh: ang: 4 (over y, x), slab: 8 (over z, core).
Axes of the slice: x: 2, y: 2, z: 4, core: 2. Of those that a mesh axis runs over, the one named last changes fastest.
Arguments:
- projections: bfloat16 [16, 1024, 2048], P('slab', 'ang'), may hold values from -6 to 6
- dest_plane: int32 [16, 1024], P('slab'), may hold values from 0 to 255, as said below
- sub_offset: int32 [16, 1024], P('slab'), may hold values from 0 to 7, as said below
- ky_bin: int32 [16, 1024], P('slab'), may hold values from 0 to 7, as said below
Outputs:
- volume_real: float32 [256, 8, 2048], P('slab', None, 'ang')
- volume_imag: float32 [256, 8, 2048], P('slab', None, 'ang')
The draws below stay inside these ranges and needn't reach their ends.
Inputs may be any that keep to these rules, and one draw needn't show every extreme that they name: With f = q for q < 512 and q - 1024 otherwise, and an integer s of 8 to 16 for each projection, e = floor(64 * 256 f / (1024 * s)) and dest_plane = floor(e / 8) + 128. Among the 2 projections of one slab index at most 512 rows fall on one aligned block of 32 planes; some slab index reaches 512. sub_offset = e mod 8 for the e of dest_plane. With f as for dest_plane and an integer r of 1 to 8 for each projection, ky_bin = floor((f + 512) r / 1024).
All inputs are finite; a program needn't handle non-finite values.
Results may differ from the reference program's by a relative error of at most 0.0085.
Values may be sent and summed in bfloat16 or wider, within the bound.
A program may use at most 192 MiB of HBM per device.

```python
import math
import jax
import jax.numpy as jnp
from jax import lax

W = 2048
H = 1024
PROJ_DEV = 2
KY = 8
REG_ITERS = 2
NPROJ = 16
NZ = 256


def cone_choice(key):
    chosen = jax.random.randint(jax.random.fold_in(key, 12), (), 0, NPROJ // PROJ_DEV)
    widest = (chosen * PROJ_DEV + PROJ_DEV + jax.random.randint(jax.random.fold_in(key, 13), (), 0, NPROJ - PROJ_DEV)) % NPROJ
    return (chosen, widest)


def row_frequency():
    row_index = jnp.arange(H, dtype=jnp.int32)
    return jnp.where(row_index < H // 2, row_index, row_index - H)


def cone_layout(key):
    slopes = jax.random.randint(jax.random.fold_in(key, 11), (NPROJ,), 8, 17)
    chosen, widest = cone_choice(key)
    proj_index = jnp.arange(NPROJ, dtype=jnp.int32)
    slopes = jnp.where(proj_index // PROJ_DEV == chosen, 16, slopes)
    slopes = jnp.where(proj_index == widest, 8, slopes)
    frequency = row_frequency()
    eighths = frequency[None, :] * (64 * NZ) // (H * slopes[:, None])
    return ((eighths // 8 + NZ // 2).astype(jnp.int32), (eighths % 8).astype(jnp.int32))


def draw_dest_plane(key, part):
    return cone_layout(key)[0]


def draw_sub_offset(key, part):
    return cone_layout(key)[1]


def draw_ky_bin(key, part):
    rates = jax.random.randint(jax.random.fold_in(key, 21), (NPROJ,), 1, KY + 1)
    chosen, widest = cone_choice(key)
    proj_index = jnp.arange(NPROJ, dtype=jnp.int32)
    rates = jnp.where(proj_index == widest, KY, rates)
    frequency = row_frequency()
    return ((frequency[None, :] + H // 2) * rates[:, None] // H).astype(jnp.int32)


def block_scale(own_key, extent, cuts, smallest, largest):
    gain, own = 1.0, jax.random.fold_in(own_key, 6)
    for position, shards_of in cuts:
        steps = jnp.exp(jax.random.uniform(jax.random.fold_in(own, position), (shards_of,), jnp.float32, smallest / len(cuts), largest / len(cuts)))
        gain = gain * jnp.repeat(steps, extent[position] // shards_of).reshape([-1 if axis == position else 1 for axis in range(len(extent))])
    return gain


def centred(rng, shape, spread, bound, shards=(), kind=jnp.bfloat16):
    entries = jax.random.normal(rng, shape, jnp.float32) * spread
    if len(shards) > 0:
        entries = block_scale(rng, shape, shards, -0.22, 0.18) * entries
    return jnp.clip(entries, min=-bound, max=bound).astype(kind)


def setup_inputs(seed: int = 0) -> dict:
    arg_keys = jax.random.split(jax.random.key(seed), 5)
    projections = centred(arg_keys[0], (NPROJ, H, W), 1.0, 6.0, ((0, 8), (1, 4)))
    dest_plane = draw_dest_plane(jax.random.fold_in(arg_keys[4], 71), 0)
    sub_offset = draw_sub_offset(jax.random.fold_in(arg_keys[4], 71), 0)
    ky_bin = draw_ky_bin(jax.random.fold_in(arg_keys[4], 71), 0)
    return dict(projections=projections, dest_plane=dest_plane, sub_offset=sub_offset, ky_bin=ky_bin)


def trig_tables(length):
    row_index = jnp.arange(length, dtype=jnp.int32)[:, None]
    column = jnp.arange(length, dtype=jnp.int32)[None, :]
    phase_angle = (row_index * column % length).astype(jnp.float32) * (2.0 * math.pi / length)
    return (jnp.cos(phase_angle).astype(jnp.bfloat16), jnp.sin(phase_angle).astype(jnp.bfloat16))

def grid_rows(buffer, centre, eighth, ky_index, rows, density):
    for shift in range(-2, 4):
        distance = shift - eighth.astype(jnp.float32) * 0.125
        weight = (jnp.exp(-0.5 * distance * distance) * density).astype(jnp.bfloat16)
        weight = lax.optimization_barrier(weight).astype(jnp.float32)
        index = (centre + (shift + 3)) * KY + ky_index
        buffer = buffer.at[index].add(weight[:, None] * rows)
    return buffer

def reference(projections, dest_plane, sub_offset, ky_bin):
    cosines_w, sines_w = trig_tables(W)
    table = jnp.concatenate([cosines_w, sines_w], axis=1)
    cosines_h, sines_h = trig_tables(H)
    unitary = 1.0 / math.sqrt(H * W)
    density = 1.0 / math.sqrt(NPROJ)

    def accumulate(volume, scan_item):
        projection_image, centre, eighth, ky_index = scan_item
        transformed = jnp.dot(projection_image, table, preferred_element_type=jnp.float32)
        row_spectra = jnp.concatenate([transformed[:, :W], -transformed[:, W:]], axis=1).astype(jnp.bfloat16)
        cosine_part = jnp.dot(cosines_h, row_spectra, preferred_element_type=jnp.float32)
        sine_part = jnp.dot(sines_h, row_spectra, preferred_element_type=jnp.float32)
        real_part = cosine_part[:, :W] + sine_part[:, W:]
        imag_part = cosine_part[:, W:] - sine_part[:, :W]
        spectral_rows = (jnp.concatenate([real_part, imag_part], axis=1) * unitary).astype(jnp.bfloat16)
        return (grid_rows(volume, centre, eighth, ky_index, spectral_rows, density), None)
    volume, unused = lax.scan(accumulate, jnp.zeros(((NZ + 6) * KY, 2 * W), jnp.float32), (projections, dest_plane, sub_offset, ky_bin))
    gridded = volume.reshape(NZ + 6, KY, 2 * W)[3:-3]
    iterate = gridded
    for sweep in range(REG_ITERS):
        bordered = jnp.pad(iterate, ((1, 1), (0, 0), (0, 0)))
        iterate = iterate - 0.25 * (iterate - gridded + (2.0 * iterate - bordered[:-2] - bordered[2:]))
    return (iterate[:, :, :W], iterate[:, :, W:])
```

```python
import functools
import math

import jax
import jax.numpy as jnp
import ml_dtypes
import numpy as np
from jax import lax
from jax.experimental import pallas as pl
from jax.experimental.pallas import tpu as pltpu
from jax.sharding import PartitionSpec as P

Z_DEV = 32
KY = 8
REG_ITERS = 2
SLOPE_LOW, SLOPE_HIGH = 8, 16
CHUNK = 256
BF16 = jnp.bfloat16
F32 = jnp.float32


def trig_values(length):
    phase = np.arange(length, dtype=np.float32) * np.float32(2.0 * math.pi / length)
    return np.cos(phase), np.sin(phase)


def column_table(width, groups):
    cos, sin = trig_values(width)
    count = width // 2 // groups
    w = np.arange(width)[:, None]
    tables = []
    for j in range(groups):
        phase = w * (groups * np.arange(count) + j)[None, :] % width
        real, imag = cos[phase], -sin[phase]
        if j == 0:
            imag[:, 0] = cos[w[:, 0] * (width // 2) % width]
        tables.append(np.concatenate([real, imag], axis=1))
    return np.stack(tables).astype(ml_dtypes.bfloat16)


def row_tables(height):
    cos, sin = trig_values(height)
    phase = np.arange(height // 2)[:, None] * np.arange(height)[None, :] % height
    cosines, sines = cos[phase], sin[phase]
    sines[0] = cos[np.arange(height) * (height // 2) % height]
    return cosines.astype(ml_dtypes.bfloat16), sines.astype(ml_dtypes.bfloat16)


def update_matrix(planes):
    eye = np.eye(planes)
    lap = 2.0 * eye - np.eye(planes, k=1) - np.eye(planes, k=-1)
    total = eye
    for sweep in range(REG_ITERS):
        total = total - 0.25 * ((total - eye) + lap @ total)
    return total.astype(ml_dtypes.bfloat16)


def placement(width, groups):
    block = width // groups
    half = block // groups
    out = np.zeros((groups, 2, groups * half, block), np.float32)
    for dest in range(groups):
        for j in range(groups):
            for m in range(half):
                if dest < groups // 2:
                    column, sign = groups * m + j, 1.0
                else:
                    column = block - (groups * m + j)
                    column, sign = (0 if j == 0 and m == 0 else column), -1.0
                out[dest, 0, j * half + m, column] = 1.0
                out[dest, 1, j * half + m, column] = sign
    return out.astype(ml_dtypes.bfloat16)


def needs(planes, height, local_count):
    half = height // 2
    per_sign = half // CHUNK
    table = np.zeros((planes // Z_DEV, 2, local_count * 2 * per_sign), np.int32)
    up = np.arange(half)
    down = np.concatenate([[-half], -np.arange(1, half)])
    mirror_up = np.concatenate([[0], -np.arange(1, half)])
    mirror_down = np.concatenate([[-half], np.arange(1, half)])
    for kind, signs in enumerate(((up, down), (mirror_up, mirror_down))):
        for sign, rows in enumerate(signs):
            for part in range(per_sign):
                f = rows[part * CHUNK : (part + 1) * CHUNK].astype(np.int64)
                reach = [(64 * planes * f // (height * s)) // 8 + planes // 2 for s in range(SLOPE_LOW, SLOPE_HIGH + 1)]
                low = np.min(reach, axis=0) - 2 - REG_ITERS
                high = np.max(reach, axis=0) + 3 + REG_ITERS
                for b in range(planes // Z_DEV):
                    hit = np.any((high >= b * Z_DEV) & (low < (b + 1) * Z_DEV))
                    for p in range(local_count):
                        table[b, kind, (p * 2 + sign) * per_sign + part] = int(hit)
    return table.reshape(-1)


def columns_kernel(x_ref, t_ref, o_ref):
    o_ref[0] = jnp.dot(x_ref[...], t_ref[0], preferred_element_type=F32).astype(o_ref.dtype)


def column_spectra(rows, table):
    groups, width, columns = table.shape
    count = rows.shape[0]
    return pl.pallas_call(
        columns_kernel,
        grid=(groups,),
        out_shape=jax.ShapeDtypeStruct((groups, count, columns), BF16),
        in_specs=[
            pl.BlockSpec((count, width), lambda j: (0, 0)),
            pl.BlockSpec((1, width, columns), lambda j: (j, 0, 0)),
        ],
        out_specs=pl.BlockSpec((1, count, columns), lambda j: (j, 0, 0)),
        compiler_params=pltpu.CompilerParams(vmem_limit_bytes=40 * 2**20),
        cost_estimate=pl.CostEstimate(
            flops=2 * count * width * columns * groups, bytes_accessed=12 * 2**20, transcendentals=0
        ),
    )(rows, table)


def grid_kernel(local_count, unitary, need_ref, r_ref, cos_ref, sin_ref, v_ref, ky_ref, o_ref, spec_d, spec_m, acc_d, acc_m):
    step = pl.program_id(0)
    half, height = cos_ref.shape
    columns = r_ref.shape[-1]
    quarter = columns // 4
    chunks = local_count * height // CHUNK

    @pl.when(step < local_count)
    def _():
        rows = r_ref[...].reshape(height, columns)
        cosine = jnp.dot(cos_ref[...], rows, preferred_element_type=F32)
        sine = jnp.dot(sin_ref[...], rows, preferred_element_type=F32)
        first = lax.broadcasted_iota(jnp.int32, (half, columns), 0) == 0
        other = jnp.where(first, sine, cosine)
        sine = jnp.where(first, 0.0, sine)
        lane = lax.broadcasted_iota(jnp.int32, (half, quarter), 1)
        packed = jnp.logical_and(lane == 0, lax.axis_index("ang") == 0)

        def part(a, i):
            return a[:, i * quarter : (i + 1) * quarter]

        for sign, (c, s) in enumerate(((cosine, sine), (other, -sine))):
            re0 = part(c, 0) + jnp.where(packed, 0.0, part(s, 2))
            im0 = jnp.where(packed, 0.0, part(c, 2)) - part(s, 0)
            re1 = part(c, 1) + part(s, 3)
            im1 = part(c, 3) - part(s, 1)
            re0m = jnp.where(packed, jnp.broadcast_to(re1[:, :1], re0.shape), re0)
            im0m = jnp.where(packed, jnp.broadcast_to(im1[:, :1], im0.shape), im0)
            re1m = jnp.where(packed, part(c, 2), re1)
            im1m = jnp.where(packed, -part(s, 2), im1)
            base = pl.multiple_of((step * 2 + sign) * half, half)
            for i, value in enumerate((re0, im0, re1, im1)):
                spec_d[pl.ds(base, half), i * quarter : (i + 1) * quarter] = (value * unitary).astype(BF16)
            for i, value in enumerate((re1m, im1m, re0m, im0m)):
                spec_m[pl.ds(base, half), i * quarter : (i + 1) * quarter] = (value * unitary).astype(BF16)

    @pl.when(step >= local_count)
    def _():
        block = step - local_count
        acc_d[...] = jnp.zeros_like(acc_d)
        acc_m[...] = jnp.zeros_like(acc_m)
        ky_row = lax.broadcasted_iota(jnp.int32, (KY, CHUNK), 0)
        for kind, (spec, acc) in enumerate(((spec_d, acc_d), (spec_m, acc_m))):
            for c in range(chunks):

                @pl.when(need_ref[(block * 2 + kind) * chunks + c] != 0)
                def _(kind=kind, spec=spec, acc=acc, c=c):
                    at = kind * chunks * CHUNK + c * CHUNK
                    weight = v_ref[:, at : at + CHUNK].astype(F32)
                    hit = ky_ref[:, at : at + CHUNK] == ky_row
                    spread = jnp.where(hit[None], weight[:, None, :], 0.0)
                    spread = spread.reshape(Z_DEV * KY, CHUNK).astype(BF16)
                    acc[...] += jnp.dot(spread, spec[c * CHUNK : (c + 1) * CHUNK, :], preferred_element_type=F32)

        for i, acc in enumerate((acc_d, acc_m)):
            for h in range(2):
                o_ref[0, i * 2 + h] = acc[:, h * 2 * quarter : (h + 1) * 2 * quarter].astype(BF16)


def gridded_blocks(received, weights, ky, planes, unitary):
    groups, local_count, quarter_rows, columns = received.shape
    height = groups * quarter_rows
    cosines, sines = row_tables(height)
    blocks = planes // Z_DEV
    chunk_count = local_count * height
    block_of = lambda i, need: (jnp.maximum(i - local_count, 0), 0)
    whole = lambda i, need: (0, 0)
    return pl.pallas_call(
        functools.partial(grid_kernel, local_count, unitary),
        out_shape=jax.ShapeDtypeStruct((blocks, 4, Z_DEV * KY, columns // 2), BF16),
        grid_spec=pltpu.PrefetchScalarGridSpec(
            num_scalar_prefetch=1,
            grid=(local_count + blocks,),
            in_specs=[
                pl.BlockSpec(
                    (groups, 1, quarter_rows, columns),
                    lambda i, need: (0, jnp.minimum(i, local_count - 1), 0, 0),
                ),
                pl.BlockSpec(cosines.shape, whole),
                pl.BlockSpec(sines.shape, whole),
                pl.BlockSpec((Z_DEV, 2 * chunk_count), block_of),
                pl.BlockSpec((1, 2 * chunk_count), whole),
            ],
            out_specs=pl.BlockSpec(
                (1, 4, Z_DEV * KY, columns // 2),
                lambda i, need: (jnp.maximum(i - local_count, 0), 0, 0, 0),
            ),
            scratch_shapes=[
                pltpu.VMEM((chunk_count, columns), BF16),
                pltpu.VMEM((chunk_count, columns), BF16),
                pltpu.VMEM((Z_DEV * KY, columns), F32),
                pltpu.VMEM((Z_DEV * KY, columns), F32),
            ],
        ),
        compiler_params=pltpu.CompilerParams(vmem_limit_bytes=48 * 2**20),
        cost_estimate=pl.CostEstimate(
            flops=2 * chunk_count * height * columns + 2 * blocks * Z_DEV * KY * chunk_count * columns,
            bytes_accessed=12 * 2**20,
            transcendentals=0,
        ),
    )(jnp.asarray(needs(planes, height, local_count)), received, jnp.asarray(cosines), jnp.asarray(sines), weights, ky)


def place_kernel(x_ref, p_ref, real_ref, imag_ref):
    groups, rows, columns = x_ref.shape
    half = columns // 2
    for i, out in enumerate((real_ref, imag_ref)):
        total = None
        for j in range(groups):
            term = jnp.dot(
                x_ref[j, :, i * half : (i + 1) * half],
                p_ref[0, i, j * half : (j + 1) * half, :],
                preferred_element_type=F32,
            )
            total = term if total is None else total + term
        out[...] = total


def placed_columns(received, table, me):
    groups, rows, columns = received.shape
    block = table.shape[-1]
    return pl.pallas_call(
        place_kernel,
        out_shape=[jax.ShapeDtypeStruct((rows, block), F32)] * 2,
        compiler_params=pltpu.CompilerParams(vmem_limit_bytes=40 * 2**20),
    )(received, lax.dynamic_slice_in_dim(table, me, 1, 0))


def slot_orders(values):
    half = values.shape[1] // 2
    low, high = values[:, :half], values[:, half:]
    back_high = high[:, :0:-1]
    direct = jnp.concatenate([low, high[:, :1], back_high], axis=1)
    mirror = jnp.concatenate([low[:, :1], back_high, high[:, :1], low[:, 1:]], axis=1)
    return jnp.concatenate([direct.reshape(1, -1), mirror.reshape(1, -1)], axis=1)


def plane_weights(dest, eighths, planes, density):
    plane = jnp.arange(planes, dtype=jnp.int32)[:, None]
    shift = plane - dest
    spread = jnp.zeros(shift.shape, BF16)
    for g in range(-2, 4):
        distance = g - eighths.astype(F32) * 0.125
        weight = (jnp.exp(-0.5 * distance * distance) * density).astype(BF16)
        spread = jnp.where(shift == g, weight, spread)
    update = jnp.asarray(update_matrix(planes))
    return jnp.dot(update, spread, preferred_element_type=F32).astype(BF16)


def on_device(projections, dest_plane, sub_offset, ky_bin):
    count_ang = lax.axis_size("ang")
    count_slab = lax.axis_size("slab")
    local_count, quarter, full_width = projections.shape
    height = quarter * count_ang
    planes = Z_DEV * count_slab
    unitary = 1.0 / math.sqrt(height * full_width)
    density = 1.0 / math.sqrt(local_count * count_slab)
    table = jnp.asarray(column_table(full_width, count_ang))
    spectra = column_spectra(projections.reshape(local_count * quarter, full_width), table)
    received = lax.all_to_all(spectra, "ang", split_axis=0, concat_axis=0, tiled=True)
    received = received.reshape(count_ang, local_count, quarter, -1)
    weights = plane_weights(slot_orders(dest_plane), slot_orders(sub_offset), planes, density)
    blocks = gridded_blocks(received, weights, slot_orders(ky_bin), planes, unitary)
    mine = lax.psum_scatter(blocks, "slab", scatter_dimension=0, tiled=True)
    mine = lax.all_to_all(mine.reshape(mine.shape[1:]), "ang", split_axis=0, concat_axis=0, tiled=True)
    real, imag = placed_columns(mine, jnp.asarray(placement(full_width, count_ang)), lax.axis_index("ang"))
    return (real.reshape(Z_DEV, KY, -1), imag.reshape(Z_DEV, KY, -1))


def solution(mesh):
    placed = (P("slab", "ang", None), P("slab", None), P("slab", None), P("slab", None))
    return jax.shard_map(
        on_device,
        mesh=mesh,
        in_specs=placed,
        out_specs=(P("slab", None, "ang"), P("slab", None, "ang")),
        check_vma=False,
    )
```

```python
import functools
import math

import jax
import jax.numpy as jnp
import ml_dtypes
import numpy as np
from jax import lax
from jax.experimental import pallas as pl
from jax.experimental.pallas import tpu as pltpu
from jax.sharding import PartitionSpec as P

Z_DEV = 32
KY = 8
REG_ITERS = 2
SLOPE_LOW, SLOPE_HIGH = 8, 16
CHUNK = 256
BF16 = jnp.bfloat16
MESH = pl.DeviceIdType.MESH
F32 = jnp.float32


def trig_values(length):
    phase = np.arange(length, dtype=np.float32) * np.float32(2.0 * math.pi / length)
    return np.cos(phase), np.sin(phase)


def column_table(width, groups):
    cos, sin = trig_values(width)
    count = width // 2 // groups
    w = np.arange(width)[:, None]
    tables = []
    for j in range(groups):
        phase = w * (groups * np.arange(count) + j)[None, :] % width
        real, imag = cos[phase], -sin[phase]
        if j == 0:
            imag[:, 0] = cos[w[:, 0] * (width // 2) % width]
        tables.append(np.concatenate([real, imag], axis=1))
    return np.stack(tables).astype(ml_dtypes.bfloat16)


def row_tables(height):
    cos, sin = trig_values(height)
    phase = np.arange(height // 2)[:, None] * np.arange(height)[None, :] % height
    cosines, sines = cos[phase], sin[phase]
    sines[0] = cos[np.arange(height) * (height // 2) % height]
    return cosines.astype(ml_dtypes.bfloat16), sines.astype(ml_dtypes.bfloat16)


def update_matrix(planes):
    eye = np.eye(planes)
    lap = 2.0 * eye - np.eye(planes, k=1) - np.eye(planes, k=-1)
    total = eye
    for sweep in range(REG_ITERS):
        total = total - 0.25 * ((total - eye) + lap @ total)
    return total.astype(ml_dtypes.bfloat16)


def placement(width, groups):
    block = width // groups
    half = block // groups
    out = np.zeros((groups, 2, groups * half, block), np.float32)
    for dest in range(groups):
        for j in range(groups):
            for m in range(half):
                if dest < groups // 2:
                    column, sign = groups * m + j, 1.0
                else:
                    column = block - (groups * m + j)
                    column, sign = (0 if j == 0 and m == 0 else column), -1.0
                out[dest, 0, j * half + m, column] = 1.0
                out[dest, 1, j * half + m, column] = sign
    return out.astype(ml_dtypes.bfloat16)


def needs(planes, height, local_count):
    half = height // 2
    per_sign = half // CHUNK
    table = np.zeros((planes // Z_DEV, 2, local_count * 2 * per_sign), np.int32)
    up = np.arange(half)
    down = np.concatenate([[-half], -np.arange(1, half)])
    mirror_up = np.concatenate([[0], -np.arange(1, half)])
    mirror_down = np.concatenate([[-half], np.arange(1, half)])
    for kind, signs in enumerate(((up, down), (mirror_up, mirror_down))):
        for sign, rows in enumerate(signs):
            for part in range(per_sign):
                f = rows[part * CHUNK : (part + 1) * CHUNK].astype(np.int64)
                reach = [(64 * planes * f // (height * s)) // 8 + planes // 2 for s in range(SLOPE_LOW, SLOPE_HIGH + 1)]
                low = np.min(reach, axis=0) - 2 - REG_ITERS
                high = np.max(reach, axis=0) + 3 + REG_ITERS
                for b in range(planes // Z_DEV):
                    hit = np.any((high >= b * Z_DEV) & (low < (b + 1) * Z_DEV))
                    for p in range(local_count):
                        table[b, kind, (p * 2 + sign) * per_sign + part] = int(hit)
    return table.reshape(-1)


def columns_kernel(x_ref, t_ref, o_ref):
    o_ref[0] = jnp.dot(x_ref[...], t_ref[0], preferred_element_type=F32).astype(o_ref.dtype)


def column_spectra(rows, table):
    groups, width, columns = table.shape
    count = rows.shape[0]
    return pl.pallas_call(
        columns_kernel,
        grid=(groups,),
        out_shape=jax.ShapeDtypeStruct((groups, count, columns), BF16),
        in_specs=[
            pl.BlockSpec((count, width), lambda j: (0, 0)),
            pl.BlockSpec((1, width, columns), lambda j: (j, 0, 0)),
        ],
        out_specs=pl.BlockSpec((1, count, columns), lambda j: (j, 0, 0)),
        compiler_params=pltpu.CompilerParams(vmem_limit_bytes=40 * 2**20),
        cost_estimate=pl.CostEstimate(
            flops=2 * count * width * columns * groups, bytes_accessed=12 * 2**20, transcendentals=0
        ),
    )(rows, table)


def grid_kernel(local_count, unitary, need_ref, r_ref, cos_ref, sin_ref, v_ref, ky_ref, o_ref, spec_d, spec_m, acc_d, acc_m):
    step = pl.program_id(0)
    half, height = cos_ref.shape
    columns = r_ref.shape[-1]
    quarter = columns // 4
    chunks = local_count * height // CHUNK

    @pl.when(step < local_count)
    def _():
        rows = r_ref[...].reshape(height, columns)
        cosine = jnp.dot(cos_ref[...], rows, preferred_element_type=F32)
        sine = jnp.dot(sin_ref[...], rows, preferred_element_type=F32)
        first = lax.broadcasted_iota(jnp.int32, (half, columns), 0) == 0
        other = jnp.where(first, sine, cosine)
        sine = jnp.where(first, 0.0, sine)
        lane = lax.broadcasted_iota(jnp.int32, (half, quarter), 1)
        packed = jnp.logical_and(lane == 0, lax.axis_index("ang") == 0)

        def part(a, i):
            return a[:, i * quarter : (i + 1) * quarter]

        for sign, (c, s) in enumerate(((cosine, sine), (other, -sine))):
            re0 = part(c, 0) + jnp.where(packed, 0.0, part(s, 2))
            im0 = jnp.where(packed, 0.0, part(c, 2)) - part(s, 0)
            re1 = part(c, 1) + part(s, 3)
            im1 = part(c, 3) - part(s, 1)
            re0m = jnp.where(packed, jnp.broadcast_to(re1[:, :1], re0.shape), re0)
            im0m = jnp.where(packed, jnp.broadcast_to(im1[:, :1], im0.shape), im0)
            re1m = jnp.where(packed, part(c, 2), re1)
            im1m = jnp.where(packed, -part(s, 2), im1)
            base = pl.multiple_of((step * 2 + sign) * half, half)
            for i, value in enumerate((re0, im0, re1, im1)):
                spec_d[pl.ds(base, half), i * quarter : (i + 1) * quarter] = (value * unitary).astype(BF16)
            for i, value in enumerate((re1m, im1m, re0m, im0m)):
                spec_m[pl.ds(base, half), i * quarter : (i + 1) * quarter] = (value * unitary).astype(BF16)

    @pl.when(step >= local_count)
    def _():
        block = step - local_count
        acc_d[...] = jnp.zeros_like(acc_d)
        acc_m[...] = jnp.zeros_like(acc_m)
        ky_row = lax.broadcasted_iota(jnp.int32, (KY, CHUNK), 0)
        for kind, (spec, acc) in enumerate(((spec_d, acc_d), (spec_m, acc_m))):
            for c in range(chunks):

                @pl.when(need_ref[(block * 2 + kind) * chunks + c] != 0)
                def _(kind=kind, spec=spec, acc=acc, c=c):
                    at = kind * chunks * CHUNK + c * CHUNK
                    weight = v_ref[:, at : at + CHUNK].astype(F32)
                    hit = ky_ref[:, at : at + CHUNK] == ky_row
                    spread = jnp.where(hit[None], weight[:, None, :], 0.0)
                    spread = spread.reshape(Z_DEV * KY, CHUNK).astype(BF16)
                    acc[...] += jnp.dot(spread, spec[c * CHUNK : (c + 1) * CHUNK, :], preferred_element_type=F32)

        for i, acc in enumerate((acc_d, acc_m)):
            for h in range(2):
                o_ref[0, i * 2 + h] = acc[:, h * 2 * quarter : (h + 1) * 2 * quarter].astype(BF16)


def gridded_blocks(received, weights, ky, planes, unitary):
    groups, local_count, quarter_rows, columns = received.shape
    height = groups * quarter_rows
    cosines, sines = row_tables(height)
    blocks = planes // Z_DEV
    chunk_count = local_count * height
    block_of = lambda i, need: (jnp.maximum(i - local_count, 0), 0)
    whole = lambda i, need: (0, 0)
    return pl.pallas_call(
        functools.partial(grid_kernel, local_count, unitary),
        out_shape=jax.ShapeDtypeStruct((blocks, 4, Z_DEV * KY, columns // 2), BF16),
        grid_spec=pltpu.PrefetchScalarGridSpec(
            num_scalar_prefetch=1,
            grid=(local_count + blocks,),
            in_specs=[
                pl.BlockSpec(
                    (groups, 1, quarter_rows, columns),
                    lambda i, need: (0, jnp.minimum(i, local_count - 1), 0, 0),
                ),
                pl.BlockSpec(cosines.shape, whole),
                pl.BlockSpec(sines.shape, whole),
                pl.BlockSpec((Z_DEV, 2 * chunk_count), block_of),
                pl.BlockSpec((1, 2 * chunk_count), whole),
            ],
            out_specs=pl.BlockSpec(
                (1, 4, Z_DEV * KY, columns // 2),
                lambda i, need: (jnp.maximum(i - local_count, 0), 0, 0, 0),
            ),
            scratch_shapes=[
                pltpu.VMEM((chunk_count, columns), BF16),
                pltpu.VMEM((chunk_count, columns), BF16),
                pltpu.VMEM((Z_DEV * KY, columns), F32),
                pltpu.VMEM((Z_DEV * KY, columns), F32),
            ],
        ),
        compiler_params=pltpu.CompilerParams(vmem_limit_bytes=48 * 2**20),
        cost_estimate=pl.CostEstimate(
            flops=2 * chunk_count * height * columns + 2 * blocks * Z_DEV * KY * chunk_count * columns,
            bytes_accessed=12 * 2**20,
            transcendentals=0,
        ),
    )(jnp.asarray(needs(planes, height, local_count)), received, jnp.asarray(cosines), jnp.asarray(sines), weights, ky)


def place_kernel(x_ref, p_ref, real_ref, imag_ref):
    groups, rows, columns = x_ref.shape
    half = columns // 2
    for i, out in enumerate((real_ref, imag_ref)):
        total = None
        for j in range(groups):
            term = jnp.dot(
                x_ref[j, :, i * half : (i + 1) * half],
                p_ref[0, i, j * half : (j + 1) * half, :],
                preferred_element_type=F32,
            )
            total = term if total is None else total + term
        out[...] = total


def placed_columns(received, table, me):
    groups, rows, columns = received.shape
    block = table.shape[-1]
    return pl.pallas_call(
        place_kernel,
        out_shape=[jax.ShapeDtypeStruct((rows, block), F32)] * 2,
        compiler_params=pltpu.CompilerParams(vmem_limit_bytes=40 * 2**20),
    )(received, lax.dynamic_slice_in_dim(table, me, 1, 0))


def reach_of(rows, planes, height):
    f = rows.astype(np.int64)
    reach = [(64 * planes * f // (height * s)) // 8 + planes // 2 for s in range(SLOPE_LOW, SLOPE_HIGH + 1)]
    low = max(int(np.min(reach)) - 2 - REG_ITERS, 0)
    high = min(int(np.max(reach)) + 3 + REG_ITERS, planes - 1)
    return low // Z_DEV, high // Z_DEV


def chunk_reach(planes, height):
    half = height // 2
    negative = -np.arange(1, half)
    up, down = np.arange(half), np.concatenate([[-half], negative])
    mirror_up, mirror_down = np.concatenate([[0], negative]), np.concatenate([[-half], -negative])
    table = []
    for order in (np.concatenate([up, down]), np.concatenate([mirror_up, mirror_down])):
        table.append([reach_of(order[i : i + CHUNK], planes, height) for i in range(0, height, CHUNK)])
    return table


def fused_kernel(
    sizes,
    x_ref,
    table_ref,
    cos_ref,
    sin_ref,
    update_ref,
    place_ref,
    index_ref,
    real_ref,
    imag_ref,
    table,
    place,
    send_a,
    recv_a,
    weights,
    acc_c,
    acc_s,
    spec_d,
    spec_m,
    acc_d,
    acc_m,
    pair_out,
    pair_in,
    total,
    from_low,
    from_high,
    got,
    table_sem,
    place_sem,
    a_send,
    a_recv,
    pair_send,
    pair_recv,
    line_send,
    low_recv,
    high_recv,
    f_send,
    f_recv,
):
    local_count, planes, chips, unitary, density = sizes
    me = lax.axis_index("ang")
    slab = lax.axis_index("slab")
    z = slab // 2
    core = slab % 2
    half, height = cos_ref.shape
    quarter_rows = height // 4
    columns = recv_a.shape[-1]
    quarter = columns // 4
    chunks = height // CHUNK
    peers = (3 - me, (me + 2) % 4, me + 1 - 2 * (me % 2), me)
    other_core = slab + 1 - 2 * core

    def table_copy(t):
        return pltpu.make_async_copy(table_ref.at[peers[t]], table.at[t], table_sem.at[t])

    place_copy = pltpu.make_async_copy(place_ref.at[me], place, place_sem)
    for t in range(4):
        table_copy(t).start()
    place_copy.start()

    barrier = pltpu.get_barrier_semaphore()
    for t in range(3):
        pl.semaphore_signal(barrier, inc=1, device_id={"ang": peers[t]}, device_id_type=MESH)
    pl.semaphore_signal(barrier, inc=1, device_id={"slab": other_core}, device_id_type=MESH)

    @pl.when(z > 0)
    def _():
        pl.semaphore_signal(barrier, inc=1, device_id={"slab": slab - 2}, device_id_type=MESH)

    @pl.when(z < chips - 1)
    def _():
        pl.semaphore_signal(barrier, inc=1, device_id={"slab": slab + 2}, device_id_type=MESH)

    at_end = jnp.logical_or(z == 0, z == chips - 1)

    @pl.when(at_end)
    def _():
        pl.semaphore_wait(barrier, 5)

    @pl.when(jnp.logical_not(at_end))
    def _():
        pl.semaphore_wait(barrier, 6)

    def a_copy(t):
        return pltpu.make_async_remote_copy(
            src_ref=send_a.at[t],
            dst_ref=recv_a.at[t],
            send_sem=a_send.at[t],
            recv_sem=a_recv.at[t],
            device_id={"ang": peers[t]},
            device_id_type=MESH,
        )

    for t in range(4):
        table_copy(t).wait()
        target = send_a if t < 3 else recv_a
        target[t] = jnp.dot(x_ref[...], table[t], preferred_element_type=F32).astype(BF16)
        if t < 3:
            a_copy(t).start()

    def weigh(i, carry):
        at = pl.ds(pl.multiple_of(i * CHUNK, CHUNK), CHUNK)
        shift = lax.broadcasted_iota(jnp.int32, (planes, CHUNK), 0) - index_ref[0:1, at]
        eighth = index_ref[1:2, at].astype(F32) * 0.125
        spread = jnp.zeros((planes, CHUNK), F32)
        for g in range(-2, 4):
            distance = g - eighth
            weight = jnp.exp(-0.5 * distance * distance) * density
            spread = jnp.where(shift == g, weight, spread)
        value = jnp.dot(update_ref[...], spread.astype(BF16), preferred_element_type=F32)
        weights[:, at] = value.astype(BF16)
        return carry

    lax.fori_loop(0, 2 * local_count * chunks, weigh, 0)

    for t in (3, 2, 1, 0):
        if t < 3:
            a_copy(t).wait()
        at = pl.ds(pl.multiple_of(peers[t] * quarter_rows, quarter_rows), quarter_rows)
        for p in range(local_count):
            rows = recv_a[t, p * quarter_rows : (p + 1) * quarter_rows, :]
            for trig, acc in ((cos_ref, acc_c), (sin_ref, acc_s)):
                term = jnp.dot(trig[:, at], rows, preferred_element_type=F32)
                acc[p] = term if t == 3 else acc[p] + term

    def finish(p, carry):
        cosine, sine = acc_c[p], acc_s[p]
        first = lax.broadcasted_iota(jnp.int32, (half, columns), 0) == 0
        other = jnp.where(first, sine, cosine)
        sine = jnp.where(first, 0.0, sine)
        lane = lax.broadcasted_iota(jnp.int32, (half, quarter), 1)
        packed = jnp.logical_and(lane == 0, me == 0)

        def part(a, i):
            return a[:, i * quarter : (i + 1) * quarter]

        for sign, (c, s) in enumerate(((cosine, sine), (other, -sine))):
            re0 = part(c, 0) + jnp.where(packed, 0.0, part(s, 2))
            im0 = jnp.where(packed, 0.0, part(c, 2)) - part(s, 0)
            re1 = part(c, 1) + part(s, 3)
            im1 = part(c, 3) - part(s, 1)
            re0m = jnp.where(packed, re1, re0)
            im0m = jnp.where(packed, im1, im0)
            re1m = jnp.where(packed, part(c, 2), re1)
            im1m = jnp.where(packed, -part(s, 2), im1)
            at = pl.ds(pl.multiple_of((p * 2 + sign) * half, half), half)
            for i, value in enumerate((re0, im0, re1, im1)):
                spec_d[at, i * quarter : (i + 1) * quarter] = (value * unitary).astype(BF16)
            for i, value in enumerate((re1m, im1m, re0m, im0m)):
                spec_m[at, i * quarter : (i + 1) * quarter] = (value * unitary).astype(BF16)
        return carry

    lax.fori_loop(0, local_count, finish, 0)

    reach = chunk_reach(planes, height)
    ky_row = lax.broadcasted_iota(jnp.int32, (KY, CHUNK), 0)

    def compute(block):
        acc_d[...] = jnp.zeros_like(acc_d)
        acc_m[...] = jnp.zeros_like(acc_m)
        plane = pl.ds(pl.multiple_of(block * Z_DEV, Z_DEV), Z_DEV)
        for kind, (spec, acc) in enumerate(((spec_d, acc_d), (spec_m, acc_m))):
            for c in range(local_count * chunks):
                low, high = reach[kind][c % chunks]

                @pl.when(jnp.logical_and(block >= low, block <= high))
                def _(kind=kind, spec=spec, acc=acc, c=c):
                    at = (kind * local_count * chunks + c) * CHUNK
                    weight = weights[plane, at : at + CHUNK].astype(F32)
                    hit = index_ref[2:3, at : at + CHUNK] == ky_row
                    spread = jnp.where(hit[None], weight[:, None, :], 0.0)
                    spread = spread.reshape(Z_DEV * KY, CHUNK).astype(BF16)
                    acc[...] += jnp.dot(spread, spec[c * CHUNK : (c + 1) * CHUNK, :], preferred_element_type=F32)

    def piece(i):
        acc = (acc_d, acc_m)[i // 2]
        return acc[:, (i % 2) * 2 * quarter : (i % 2 + 1) * 2 * quarter]

    def order(t):
        middle = jnp.where(t > 0, (t + 1) % 3 + 1, 0)
        base = jnp.where(jnp.logical_or(z == 0, z == chips - 1), t, middle)
        return jnp.where(z >= chips // 2, base, chips - 1 - base)

    def pair_copy(t):
        return pltpu.make_async_remote_copy(
            src_ref=pair_out.at[t],
            dst_ref=pair_in.at[t],
            send_sem=pair_send.at[t],
            recv_sem=pair_recv.at[t],
            device_id={"slab": other_core},
            device_id_type=MESH,
        )

    def line_copy(t, owner, up):
        buffer, sem = (from_low, low_recv) if up else (from_high, high_recv)
        return pltpu.make_async_remote_copy(
            src_ref=total.at[t],
            dst_ref=buffer.at[owner],
            send_sem=line_send.at[t],
            recv_sem=sem.at[owner],
            device_id={"slab": slab + 2 if up else slab - 2},
            device_id_type=MESH,
        )

    def add(t, buffer, owner):
        total[t] = (total[t].astype(F32) + buffer[owner].astype(F32)).astype(BF16)

    def forward(t):
        owner = order(t)

        @pl.when(owner > z)
        def _():
            @pl.when(z > 0)
            def _():
                line_copy(t, owner, True).wait_recv()
                add(t, from_low, owner)

            line_copy(t, owner, True).start()

        @pl.when(owner < z)
        def _():
            @pl.when(z < chips - 1)
            def _():
                line_copy(t, owner, False).wait_recv()
                add(t, from_high, owner)

            line_copy(t, owner, False).start()

    def step(t, carry):
        owner = order(t)
        compute(owner * 2 + 1 - core)
        for i in range(4):
            pair_out[t, i] = piece(i).astype(BF16)
        pair_copy(t).start()
        compute(owner * 2 + core)
        pair_copy(t).wait_recv()
        for i in range(4):
            total[t, i] = (piece(i) + pair_in[t, i].astype(F32)).astype(BF16)

        @pl.when(jnp.logical_and(at_end, t < chips - 1))
        def _():
            forward(t)

        @pl.when(jnp.logical_and(jnp.logical_not(at_end), t > 0))
        def _():
            forward(t - 1)

        return carry

    lax.fori_loop(0, chips, step, 0)

    last = chips - 1

    @pl.when(z > 0)
    def _():
        line_copy(last, z, True).wait_recv()
        add(last, from_low, z)

    @pl.when(z < chips - 1)
    def _():
        line_copy(last, z, False).wait_recv()
        add(last, from_high, z)

    def f_copy(t):
        return pltpu.make_async_remote_copy(
            src_ref=total.at[last, peers[t]],
            dst_ref=got.at[t],
            send_sem=f_send.at[t],
            recv_sem=f_recv.at[t],
            device_id={"ang": peers[t]},
            device_id_type=MESH,
        )

    for t in range(3):
        f_copy(t).start()
    place_copy.wait()
    for t in (3, 2, 1, 0):
        if t < 3:
            f_copy(t).wait()
        value = total[last, me] if t == 3 else got[t]
        at = pl.ds(pl.multiple_of(peers[t] * quarter, quarter), quarter)
        for i, out in enumerate((real_ref, imag_ref)):
            term = jnp.dot(value[:, i * quarter : (i + 1) * quarter], place[i, at, :], preferred_element_type=F32)
            if t == 3:
                out[...] = term
            else:
                out[...] += term

    def drain(t, carry):
        pair_copy(t).wait_send()

        @pl.when(t < last)
        def _():
            line_copy(t, 0, True).wait_send()

        return carry

    lax.fori_loop(0, chips, drain, 0)


def fused(rows, indices, local_count, planes, chips, height, unitary, density):
    count, width = rows.shape
    table = jnp.asarray(column_table(width, 4))
    columns = table.shape[-1]
    cosines, sines = row_tables(height)
    places = jnp.asarray(placement(width, 4))
    block = (4, Z_DEV * KY, columns // 2)
    slots = local_count * height
    vmem = pl.BlockSpec(memory_space=pltpu.VMEM)
    anywhere = pl.BlockSpec(memory_space=pl.ANY)
    dma = pltpu.SemaphoreType.DMA
    return pl.pallas_call(
        functools.partial(fused_kernel, (local_count, planes, chips, unitary, density)),
        out_shape=[jax.ShapeDtypeStruct((Z_DEV * KY, width // 4), F32)] * 2,
        in_specs=[vmem, anywhere, vmem, vmem, vmem, anywhere, vmem],
        out_specs=[vmem, vmem],
        scratch_shapes=[
            pltpu.VMEM(table.shape, BF16),
            pltpu.VMEM(places.shape[1:], BF16),
            pltpu.VMEM((3, count, columns), BF16),
            pltpu.VMEM((4, count, columns), BF16),
            pltpu.VMEM((planes, 2 * slots), BF16),
            pltpu.VMEM((local_count, height // 2, columns), F32),
            pltpu.VMEM((local_count, height // 2, columns), F32),
            pltpu.VMEM((slots, columns), BF16),
            pltpu.VMEM((slots, columns), BF16),
            pltpu.VMEM((Z_DEV * KY, columns), F32),
            pltpu.VMEM((Z_DEV * KY, columns), F32),
            pltpu.VMEM((chips,) + block, BF16),
            pltpu.VMEM((chips,) + block, BF16),
            pltpu.VMEM((chips,) + block, BF16),
            pltpu.VMEM((chips,) + block, BF16),
            pltpu.VMEM((chips,) + block, BF16),
            pltpu.VMEM((3,) + block[1:], BF16),
            dma((4,)),
            dma,
            dma((3,)),
            dma((3,)),
            dma((chips,)),
            dma((chips,)),
            dma((chips,)),
            dma((chips,)),
            dma((chips,)),
            dma((3,)),
            dma((3,)),
        ],
        compiler_params=pltpu.CompilerParams(
            collective_id=0, has_side_effects=True, vmem_limit_bytes=58 * 2**20
        ),
        cost_estimate=pl.CostEstimate(flops=14 * 10**9, bytes_accessed=20 * 2**20, transcendentals=0),
    )(
        rows,
        table,
        jnp.asarray(cosines),
        jnp.asarray(sines),
        jnp.asarray(update_matrix(planes)),
        places,
        indices,
    )


def slot_orders(values):
    half = values.shape[1] // 2
    low, high = values[:, :half], values[:, half:]
    back_high = high[:, :0:-1]
    direct = jnp.concatenate([low, high[:, :1], back_high], axis=1)
    mirror = jnp.concatenate([low[:, :1], back_high, high[:, :1], low[:, 1:]], axis=1)
    return jnp.concatenate([direct.reshape(1, -1), mirror.reshape(1, -1)], axis=1)


def plane_weights(dest, eighths, planes, density):
    plane = jnp.arange(planes, dtype=jnp.int32)[:, None]
    shift = plane - dest
    spread = jnp.zeros(shift.shape, BF16)
    for g in range(-2, 4):
        distance = g - eighths.astype(F32) * 0.125
        weight = (jnp.exp(-0.5 * distance * distance) * density).astype(BF16)
        spread = jnp.where(shift == g, weight, spread)
    update = jnp.asarray(update_matrix(planes))
    return jnp.dot(update, spread, preferred_element_type=F32).astype(BF16)


def on_device(projections, dest_plane, sub_offset, ky_bin):
    count_ang = lax.axis_size("ang")
    count_slab = lax.axis_size("slab")
    local_count, quarter, full_width = projections.shape
    height = quarter * count_ang
    planes = Z_DEV * count_slab
    unitary = 1.0 / math.sqrt(height * full_width)
    density = 1.0 / math.sqrt(local_count * count_slab)
    if count_ang == 4 and count_slab == 8:
        indices = jnp.concatenate([slot_orders(dest_plane), slot_orders(sub_offset), slot_orders(ky_bin)], axis=0)
        real, imag = fused(
            projections.reshape(local_count * quarter, full_width),
            indices,
            local_count,
            planes,
            count_slab // 2,
            height,
            unitary,
            density,
        )
        return (real.reshape(Z_DEV, KY, -1), imag.reshape(Z_DEV, KY, -1))
    table = jnp.asarray(column_table(full_width, count_ang))
    spectra = column_spectra(projections.reshape(local_count * quarter, full_width), table)
    received = lax.all_to_all(spectra, "ang", split_axis=0, concat_axis=0, tiled=True)
    received = received.reshape(count_ang, local_count, quarter, -1)
    weights = plane_weights(slot_orders(dest_plane), slot_orders(sub_offset), planes, density)
    blocks = gridded_blocks(received, weights, slot_orders(ky_bin), planes, unitary)
    mine = lax.psum_scatter(blocks, "slab", scatter_dimension=0, tiled=True)
    mine = lax.all_to_all(mine.reshape(mine.shape[1:]), "ang", split_axis=0, concat_axis=0, tiled=True)
    real, imag = placed_columns(mine, jnp.asarray(placement(full_width, count_ang)), lax.axis_index("ang"))
    return (real.reshape(Z_DEV, KY, -1), imag.reshape(Z_DEV, KY, -1))


def solution(mesh):
    placed = (P("slab", "ang", None), P("slab", None), P("slab", None), P("slab", None))
    return jax.shard_map(
        on_device,
        mesh=mesh,
        in_specs=placed,
        out_specs=(P("slab", None, "ang"), P("slab", None, "ang")),
        check_vma=False,
    )
```

```python
import functools
import math

import jax
import jax.numpy as jnp
import ml_dtypes
import numpy as np
from jax import lax
from jax.experimental import pallas as pl
from jax.experimental.pallas import tpu as pltpu
from jax.sharding import PartitionSpec as P

Z_DEV = 32
KY = 8
REG_ITERS = 2
SLOPE_LOW, SLOPE_HIGH = 8, 16
CHUNK = 256
BF16 = jnp.bfloat16
MESH = pl.DeviceIdType.MESH
F32 = jnp.float32


def trig_values(length):
    phase = np.arange(length, dtype=np.float32) * np.float32(2.0 * math.pi / length)
    return np.cos(phase), np.sin(phase)


def column_table(width, groups):
    cos, sin = trig_values(width)
    count = width // 2 // groups
    w = np.arange(width)[:, None]
    tables = []
    for j in range(groups):
        phase = w * (groups * np.arange(count) + j)[None, :] % width
        real, imag = cos[phase], -sin[phase]
        if j == 0:
            imag[:, 0] = cos[w[:, 0] * (width // 2) % width]
        tables.append(np.concatenate([real, imag], axis=1))
    return np.stack(tables).astype(ml_dtypes.bfloat16)


def row_tables(height):
    cos, sin = trig_values(height)
    phase = np.arange(height // 2)[:, None] * np.arange(height)[None, :] % height
    cosines, sines = cos[phase], sin[phase]
    sines[0] = cos[np.arange(height) * (height // 2) % height]
    return cosines.astype(ml_dtypes.bfloat16), sines.astype(ml_dtypes.bfloat16)


def update_matrix(planes):
    eye = np.eye(planes)
    lap = 2.0 * eye - np.eye(planes, k=1) - np.eye(planes, k=-1)
    total = eye
    for sweep in range(REG_ITERS):
        total = total - 0.25 * ((total - eye) + lap @ total)
    return total.astype(ml_dtypes.bfloat16)


def placement(width, groups):
    block = width // groups
    half = block // groups
    out = np.zeros((groups, 2, groups * half, block), np.float32)
    for dest in range(groups):
        for j in range(groups):
            for m in range(half):
                if dest < groups // 2:
                    column, sign = groups * m + j, 1.0
                else:
                    column = block - (groups * m + j)
                    column, sign = (0 if j == 0 and m == 0 else column), -1.0
                out[dest, 0, j * half + m, column] = 1.0
                out[dest, 1, j * half + m, column] = sign
    return out.astype(ml_dtypes.bfloat16)


def needs(planes, height, local_count):
    half = height // 2
    per_sign = half // CHUNK
    table = np.zeros((planes // Z_DEV, 2, local_count * 2 * per_sign), np.int32)
    up = np.arange(half)
    down = np.concatenate([[-half], -np.arange(1, half)])
    mirror_up = np.concatenate([[0], -np.arange(1, half)])
    mirror_down = np.concatenate([[-half], np.arange(1, half)])
    for kind, signs in enumerate(((up, down), (mirror_up, mirror_down))):
        for sign, rows in enumerate(signs):
            for part in range(per_sign):
                f = rows[part * CHUNK : (part + 1) * CHUNK].astype(np.int64)
                reach = [(64 * planes * f // (height * s)) // 8 + planes // 2 for s in range(SLOPE_LOW, SLOPE_HIGH + 1)]
                low = np.min(reach, axis=0) - 2 - REG_ITERS
                high = np.max(reach, axis=0) + 3 + REG_ITERS
                for b in range(planes // Z_DEV):
                    hit = np.any((high >= b * Z_DEV) & (low < (b + 1) * Z_DEV))
                    for p in range(local_count):
                        table[b, kind, (p * 2 + sign) * per_sign + part] = int(hit)
    return table.reshape(-1)


def columns_kernel(x_ref, t_ref, o_ref):
    o_ref[0] = jnp.dot(x_ref[...], t_ref[0], preferred_element_type=F32).astype(o_ref.dtype)


def column_spectra(rows, table):
    groups, width, columns = table.shape
    count = rows.shape[0]
    return pl.pallas_call(
        columns_kernel,
        grid=(groups,),
        out_shape=jax.ShapeDtypeStruct((groups, count, columns), BF16),
        in_specs=[
            pl.BlockSpec((count, width), lambda j: (0, 0)),
            pl.BlockSpec((1, width, columns), lambda j: (j, 0, 0)),
        ],
        out_specs=pl.BlockSpec((1, count, columns), lambda j: (j, 0, 0)),
        compiler_params=pltpu.CompilerParams(vmem_limit_bytes=40 * 2**20),
        cost_estimate=pl.CostEstimate(
            flops=2 * count * width * columns * groups, bytes_accessed=12 * 2**20, transcendentals=0
        ),
    )(rows, table)


def grid_kernel(local_count, unitary, need_ref, r_ref, cos_ref, sin_ref, v_ref, ky_ref, o_ref, spec_d, spec_m, acc_d, acc_m):
    step = pl.program_id(0)
    half, height = cos_ref.shape
    columns = r_ref.shape[-1]
    quarter = columns // 4
    chunks = local_count * height // CHUNK

    @pl.when(step < local_count)
    def _():
        rows = r_ref[...].reshape(height, columns)
        cosine = jnp.dot(cos_ref[...], rows, preferred_element_type=F32)
        sine = jnp.dot(sin_ref[...], rows, preferred_element_type=F32)
        first = lax.broadcasted_iota(jnp.int32, (half, columns), 0) == 0
        other = jnp.where(first, sine, cosine)
        sine = jnp.where(first, 0.0, sine)
        lane = lax.broadcasted_iota(jnp.int32, (half, quarter), 1)
        packed = jnp.logical_and(lane == 0, lax.axis_index("ang") == 0)

        def part(a, i):
            return a[:, i * quarter : (i + 1) * quarter]

        for sign, (c, s) in enumerate(((cosine, sine), (other, -sine))):
            re0 = part(c, 0) + jnp.where(packed, 0.0, part(s, 2))
            im0 = jnp.where(packed, 0.0, part(c, 2)) - part(s, 0)
            re1 = part(c, 1) + part(s, 3)
            im1 = part(c, 3) - part(s, 1)
            re0m = jnp.where(packed, jnp.broadcast_to(re1[:, :1], re0.shape), re0)
            im0m = jnp.where(packed, jnp.broadcast_to(im1[:, :1], im0.shape), im0)
            re1m = jnp.where(packed, part(c, 2), re1)
            im1m = jnp.where(packed, -part(s, 2), im1)
            base = pl.multiple_of((step * 2 + sign) * half, half)
            for i, value in enumerate((re0, im0, re1, im1)):
                spec_d[pl.ds(base, half), i * quarter : (i + 1) * quarter] = (value * unitary).astype(BF16)
            for i, value in enumerate((re1m, im1m, re0m, im0m)):
                spec_m[pl.ds(base, half), i * quarter : (i + 1) * quarter] = (value * unitary).astype(BF16)

    @pl.when(step >= local_count)
    def _():
        block = step - local_count
        acc_d[...] = jnp.zeros_like(acc_d)
        acc_m[...] = jnp.zeros_like(acc_m)
        ky_row = lax.broadcasted_iota(jnp.int32, (KY, CHUNK), 0)
        for kind, (spec, acc) in enumerate(((spec_d, acc_d), (spec_m, acc_m))):
            for c in range(chunks):

                @pl.when(need_ref[(block * 2 + kind) * chunks + c] != 0)
                def _(kind=kind, spec=spec, acc=acc, c=c):
                    at = kind * chunks * CHUNK + c * CHUNK
                    weight = v_ref[:, at : at + CHUNK].astype(F32)
                    hit = ky_ref[:, at : at + CHUNK] == ky_row
                    spread = jnp.where(hit[None], weight[:, None, :], 0.0)
                    spread = spread.reshape(Z_DEV * KY, CHUNK).astype(BF16)
                    acc[...] += jnp.dot(spread, spec[c * CHUNK : (c + 1) * CHUNK, :], preferred_element_type=F32)

        for i, acc in enumerate((acc_d, acc_m)):
            for h in range(2):
                o_ref[0, i * 2 + h] = acc[:, h * 2 * quarter : (h + 1) * 2 * quarter].astype(BF16)


def gridded_blocks(received, weights, ky, planes, unitary):
    groups, local_count, quarter_rows, columns = received.shape
    height = groups * quarter_rows
    cosines, sines = row_tables(height)
    blocks = planes // Z_DEV
    chunk_count = local_count * height
    block_of = lambda i, need: (jnp.maximum(i - local_count, 0), 0)
    whole = lambda i, need: (0, 0)
    return pl.pallas_call(
        functools.partial(grid_kernel, local_count, unitary),
        out_shape=jax.ShapeDtypeStruct((blocks, 4, Z_DEV * KY, columns // 2), BF16),
        grid_spec=pltpu.PrefetchScalarGridSpec(
            num_scalar_prefetch=1,
            grid=(local_count + blocks,),
            in_specs=[
                pl.BlockSpec(
                    (groups, 1, quarter_rows, columns),
                    lambda i, need: (0, jnp.minimum(i, local_count - 1), 0, 0),
                ),
                pl.BlockSpec(cosines.shape, whole),
                pl.BlockSpec(sines.shape, whole),
                pl.BlockSpec((Z_DEV, 2 * chunk_count), block_of),
                pl.BlockSpec((1, 2 * chunk_count), whole),
            ],
            out_specs=pl.BlockSpec(
                (1, 4, Z_DEV * KY, columns // 2),
                lambda i, need: (jnp.maximum(i - local_count, 0), 0, 0, 0),
            ),
            scratch_shapes=[
                pltpu.VMEM((chunk_count, columns), BF16),
                pltpu.VMEM((chunk_count, columns), BF16),
                pltpu.VMEM((Z_DEV * KY, columns), F32),
                pltpu.VMEM((Z_DEV * KY, columns), F32),
            ],
        ),
        compiler_params=pltpu.CompilerParams(vmem_limit_bytes=48 * 2**20),
        cost_estimate=pl.CostEstimate(
            flops=2 * chunk_count * height * columns + 2 * blocks * Z_DEV * KY * chunk_count * columns,
            bytes_accessed=12 * 2**20,
            transcendentals=0,
        ),
    )(jnp.asarray(needs(planes, height, local_count)), received, jnp.asarray(cosines), jnp.asarray(sines), weights, ky)


def place_kernel(x_ref, p_ref, real_ref, imag_ref):
    groups, rows, columns = x_ref.shape
    half = columns // 2
    for i, out in enumerate((real_ref, imag_ref)):
        total = None
        for j in range(groups):
            term = jnp.dot(
                x_ref[j, :, i * half : (i + 1) * half],
                p_ref[0, i, j * half : (j + 1) * half, :],
                preferred_element_type=F32,
            )
            total = term if total is None else total + term
        out[...] = total


def placed_columns(received, table, me):
    groups, rows, columns = received.shape
    block = table.shape[-1]
    return pl.pallas_call(
        place_kernel,
        out_shape=[jax.ShapeDtypeStruct((rows, block), F32)] * 2,
        compiler_params=pltpu.CompilerParams(vmem_limit_bytes=40 * 2**20),
    )(received, lax.dynamic_slice_in_dim(table, me, 1, 0))


def fused_kernel(
    sizes,
    x_ref,
    table_ref,
    cos_ref,
    sin_ref,
    update_ref,
    dest_ref,
    eighth_ref,
    ky_ref,
    out_ref,
    table,
    index_ref,
    send_a,
    recv_a,
    weights,
    acc_c,
    acc_s,
    spec_d,
    spec_m,
    spread,
    pair_out,
    pair_in,
    total,
    from_low,
    from_high,
    own,
    got,
    table_sem,
    a_send,
    a_recv,
    pair_send,
    pair_recv,
    line_send,
    low_recv,
    high_recv,
    f_send,
    f_recv,
):
    local_count, planes, chips, unitary, density = sizes
    me = lax.axis_index("ang")
    slab = lax.axis_index("slab")
    z = slab // 2
    core = slab % 2
    half, height = cos_ref.shape
    quarter_rows = height // 4
    columns = recv_a.shape[-1]
    quarter = columns // 4
    chunks = height // CHUNK
    peers = (3 - me, (me + 2) % 4, me + 1 - 2 * (me % 2), me)
    other_core = slab + 1 - 2 * core

    def table_copy(t):
        return pltpu.make_async_copy(table_ref.at[peers[t]], table.at[t], table_sem.at[t])

    for t in range(4):
        table_copy(t).start()

    barrier = pltpu.get_barrier_semaphore()
    for t in range(3):
        pl.semaphore_signal(barrier, inc=1, device_id={"ang": peers[t]}, device_id_type=MESH)
    pl.semaphore_signal(barrier, inc=1, device_id={"slab": other_core}, device_id_type=MESH)

    @pl.when(z > 0)
    def _():
        pl.semaphore_signal(barrier, inc=1, device_id={"slab": slab - 2}, device_id_type=MESH)

    @pl.when(z < chips - 1)
    def _():
        pl.semaphore_signal(barrier, inc=1, device_id={"slab": slab + 2}, device_id_type=MESH)

    at_end = jnp.logical_or(z == 0, z == chips - 1)

    @pl.when(at_end)
    def _():
        pl.semaphore_wait(barrier, 5)

    @pl.when(jnp.logical_not(at_end))
    def _():
        pl.semaphore_wait(barrier, 6)

    def a_copy(t):
        return pltpu.make_async_remote_copy(
            src_ref=send_a.at[t],
            dst_ref=recv_a.at[t],
            send_sem=a_send.at[t],
            recv_sem=a_recv.at[t],
            device_id={"ang": peers[t]},
            device_id_type=MESH,
        )

    for t in range(4):
        table_copy(t).wait()
        target = send_a if t < 3 else recv_a
        target[t] = jnp.dot(x_ref[...], table[t], preferred_element_type=F32).astype(BF16)
        if t < 3:
            a_copy(t).start()

    held = 8
    raw = jnp.concatenate([dest_ref[...], eighth_ref[...], ky_ref[...]], axis=0)
    raw = jnp.concatenate([raw, jnp.zeros((held - raw.shape[0], height), jnp.int32)], axis=0)
    low, high = raw[:, :half], raw[:, half:]
    row = lax.broadcasted_iota(jnp.int32, (half, half), 0)
    flip = (row + lax.broadcasted_iota(jnp.int32, (half, half), 1) == half).astype(F32).astype(BF16)
    back = jnp.dot(high.astype(F32).astype(BF16), flip, preferred_element_type=F32).astype(jnp.int32)
    lane_0 = lax.broadcasted_iota(jnp.int32, (held, half), 1) == 0
    low_0 = jnp.broadcast_to(low[:, :1], low.shape)
    high_0 = jnp.broadcast_to(high[:, :1], high.shape)
    orders = (
        low,
        jnp.where(lane_0, high_0, back),
        jnp.where(lane_0, low_0, back),
        jnp.where(lane_0, high_0, low),
    )
    for kind in range(2):
        for p in range(local_count):
            for sign in range(2):
                at = ((kind * local_count + p) * 2 + sign) * half
                for i in range(3):
                    source = i * local_count + p
                    index_ref[i : i + 1, at : at + half] = orders[kind * 2 + sign][source : source + 1, :]

    def weigh(i, carry):
        at = pl.ds(pl.multiple_of(i * CHUNK, CHUNK), CHUNK)
        shift = lax.broadcasted_iota(jnp.int32, (planes, CHUNK), 0) - index_ref[0:1, at]
        eighth = index_ref[1:2, at].astype(F32) * 0.125
        window = jnp.zeros((planes, CHUNK), F32)
        for g in range(-2, 4):
            distance = g - eighth
            weight = jnp.exp(-0.5 * distance * distance) * density
            window = jnp.where(shift == g, weight, window)
        value = jnp.dot(update_ref[...], window.astype(BF16), preferred_element_type=F32)
        weights[...] = value
        hit = index_ref[2:3, at] == lax.broadcasted_iota(jnp.int32, (KY, CHUNK), 0)

        def scatter(block, inner):
            plane = pl.ds(pl.multiple_of(block * Z_DEV, Z_DEV), Z_DEV)
            cells = jnp.where(hit[None], weights[plane, :][:, None, :], 0.0)
            spread[block, :, at] = cells.reshape(Z_DEV * KY, CHUNK).astype(BF16)
            return inner

        lax.fori_loop(0, planes // Z_DEV, scatter, 0)
        return carry

    lax.fori_loop(0, 2 * local_count * chunks, weigh, 0)

    for t in (3, 2, 1, 0):
        if t < 3:
            a_copy(t).wait()
        at = pl.ds(pl.multiple_of(peers[t] * quarter_rows, quarter_rows), quarter_rows)
        for p in range(local_count):
            rows = recv_a[t, p * quarter_rows : (p + 1) * quarter_rows, :]
            for trig, acc in ((cos_ref, acc_c), (sin_ref, acc_s)):
                term = jnp.dot(trig[:, at], rows, preferred_element_type=F32)
                acc[p] = term if t == 3 else acc[p] + term

    def finish(p, carry):
        cosine, sine = acc_c[p], acc_s[p]
        first = lax.broadcasted_iota(jnp.int32, (half, columns), 0) == 0
        other = jnp.where(first, sine, cosine)
        sine = jnp.where(first, 0.0, sine)
        lane = lax.broadcasted_iota(jnp.int32, (half, quarter), 1)
        packed = jnp.logical_and(lane == 0, me == 0)

        def part(a, i):
            return a[:, i * quarter : (i + 1) * quarter]

        for sign, (c, s) in enumerate(((cosine, sine), (other, -sine))):
            re0 = part(c, 0) + jnp.where(packed, 0.0, part(s, 2))
            im0 = jnp.where(packed, 0.0, part(c, 2)) - part(s, 0)
            re1 = part(c, 1) + part(s, 3)
            im1 = part(c, 3) - part(s, 1)
            re0m = jnp.where(packed, re1, re0)
            im0m = jnp.where(packed, im1, im0)
            re1m = jnp.where(packed, part(c, 2), re1)
            im1m = jnp.where(packed, -part(s, 2), im1)
            at = pl.ds(pl.multiple_of((p * 2 + sign) * half, half), half)
            for i, value in enumerate((re0, im0, re1, im1)):
                spec_d[at, i * quarter : (i + 1) * quarter] = (value * unitary).astype(BF16)
            for i, value in enumerate((re1m, im1m, re0m, im0m)):
                spec_m[at, i * quarter : (i + 1) * quarter] = (value * unitary).astype(BF16)
        return carry

    lax.fori_loop(0, local_count, finish, 0)

    slots = local_count * height

    def piece(block, i):
        kind, side = i // 2, i % 2
        spec = (spec_d, spec_m)[kind]
        return jnp.dot(
            spread[block, :, kind * slots : (kind + 1) * slots],
            spec[:, side * 2 * quarter : (side + 1) * 2 * quarter],
            preferred_element_type=F32,
        )

    def order(t):
        middle = jnp.where(t > 0, (t + 1) % 3 + 1, 0)
        base = jnp.where(jnp.logical_or(z == 0, z == chips - 1), t, middle)
        return jnp.where(z >= chips // 2, base, chips - 1 - base)

    def pair_copy(t):
        return pltpu.make_async_remote_copy(
            src_ref=pair_out.at[t],
            dst_ref=pair_in.at[t],
            send_sem=pair_send.at[t],
            recv_sem=pair_recv.at[t],
            device_id={"slab": other_core},
            device_id_type=MESH,
        )

    def line_copy(t, owner, up):
        buffer, sem = (from_low, low_recv) if up else (from_high, high_recv)
        return pltpu.make_async_remote_copy(
            src_ref=total.at[t],
            dst_ref=buffer.at[owner],
            send_sem=line_send.at[t],
            recv_sem=sem.at[owner],
            device_id={"slab": slab + 2 if up else slab - 2},
            device_id_type=MESH,
        )

    def add(t, buffer, owner):
        total[t] = (total[t].astype(F32) + buffer[owner].astype(F32)).astype(BF16)

    def forward(t):
        owner = order(t)

        @pl.when(owner > z)
        def _():
            @pl.when(z > 0)
            def _():
                line_copy(t, owner, True).wait_recv()
                add(t, from_low, owner)

            line_copy(t, owner, True).start()

        @pl.when(owner < z)
        def _():
            @pl.when(z < chips - 1)
            def _():
                line_copy(t, owner, False).wait_recv()
                add(t, from_high, owner)

            line_copy(t, owner, False).start()

    def step(t, carry):
        owner = order(t)
        for i in range(4):
            pair_out[t, i] = piece(owner * 2 + 1 - core, i).astype(BF16)
        pair_copy(t).start()
        for i in range(4):
            own[i] = piece(owner * 2 + core, i)
        pair_copy(t).wait_recv()
        for i in range(4):
            total[t, i] = (own[i] + pair_in[t, i].astype(F32)).astype(BF16)

        @pl.when(jnp.logical_and(at_end, t < chips - 1))
        def _():
            forward(t)

        @pl.when(jnp.logical_and(jnp.logical_not(at_end), t > 0))
        def _():
            forward(t - 1)

        return carry

    lax.fori_loop(0, chips, step, 0)

    last = chips - 1

    @pl.when(z > 0)
    def _():
        line_copy(last, z, True).wait_recv()
        add(last, from_low, z)

    @pl.when(z < chips - 1)
    def _():
        line_copy(last, z, False).wait_recv()
        add(last, from_high, z)

    def f_copy(t):
        return pltpu.make_async_remote_copy(
            src_ref=total.at[last, peers[t]],
            dst_ref=got.at[t],
            send_sem=f_send.at[t],
            recv_sem=f_recv.at[t],
            device_id={"ang": peers[t]},
            device_id_type=MESH,
        )

    for t in range(3):
        f_copy(t).start()
    out_ref[3] = total[last, me]
    for t in range(3):
        f_copy(t).wait()
        out_ref[t] = got[t]

    def drain(t, carry):
        pair_copy(t).wait_send()

        @pl.when(t < last)
        def _():
            line_copy(t, 0, True).wait_send()

        return carry

    lax.fori_loop(0, chips, drain, 0)


def fused(rows, dest, eighths, ky, local_count, planes, chips, height, unitary, density):
    count, width = rows.shape
    table = jnp.asarray(column_table(width, 4))
    columns = table.shape[-1]
    cosines, sines = row_tables(height)
    block = (4, Z_DEV * KY, columns // 2)
    slots = local_count * height
    vmem = pl.BlockSpec(memory_space=pltpu.VMEM)
    anywhere = pl.BlockSpec(memory_space=pl.ANY)
    dma = pltpu.SemaphoreType.DMA
    return pl.pallas_call(
        functools.partial(fused_kernel, (local_count, planes, chips, unitary, density)),
        out_shape=jax.ShapeDtypeStruct(block, BF16),
        in_specs=[vmem, anywhere, vmem, vmem, vmem, vmem, vmem, vmem],
        out_specs=vmem,
        scratch_shapes=[
            pltpu.VMEM(table.shape, BF16),
            pltpu.VMEM((8, 2 * slots), jnp.int32),
            pltpu.VMEM((3, count, columns), BF16),
            pltpu.VMEM((4, count, columns), BF16),
            pltpu.VMEM((planes, CHUNK), F32),
            pltpu.VMEM((local_count, height // 2, columns), F32),
            pltpu.VMEM((local_count, height // 2, columns), F32),
            pltpu.VMEM((slots, columns), BF16),
            pltpu.VMEM((slots, columns), BF16),
            pltpu.VMEM((planes // Z_DEV, Z_DEV * KY, 2 * slots), BF16),
            pltpu.VMEM((chips,) + block, BF16),
            pltpu.VMEM((chips,) + block, BF16),
            pltpu.VMEM((chips,) + block, BF16),
            pltpu.VMEM((chips,) + block, BF16),
            pltpu.VMEM((chips,) + block, BF16),
            pltpu.VMEM(block, F32),
            pltpu.VMEM((3,) + block[1:], BF16),
            dma((4,)),
            dma((3,)),
            dma((3,)),
            dma((chips,)),
            dma((chips,)),
            dma((chips,)),
            dma((chips,)),
            dma((chips,)),
            dma((3,)),
            dma((3,)),
        ],
        compiler_params=pltpu.CompilerParams(
            collective_id=0, has_side_effects=True, vmem_limit_bytes=58 * 2**20
        ),
        cost_estimate=pl.CostEstimate(flops=14 * 10**9, bytes_accessed=20 * 2**20, transcendentals=0),
    )(
        rows,
        table,
        jnp.asarray(cosines),
        jnp.asarray(sines),
        jnp.asarray(update_matrix(planes)),
        dest,
        eighths,
        ky,
    )


def gathered_kernel(x_ref, place_ref, real_ref, imag_ref, place, sem):
    me = lax.axis_index("ang")
    copy = pltpu.make_async_copy(place_ref.at[me], place, sem)
    copy.start()
    peers = (3 - me, (me + 2) % 4, me + 1 - 2 * (me % 2), me)
    half = x_ref.shape[-1] // 2
    copy.wait()
    for i, out in enumerate((real_ref, imag_ref)):
        total = None
        for t in range(4):
            at = pl.ds(pl.multiple_of(peers[t] * half, half), half)
            term = jnp.dot(x_ref[t, :, i * half : (i + 1) * half], place[i, at, :], preferred_element_type=F32)
            total = term if total is None else total + term
        out[...] = total


def gathered_columns(received, table):
    rows, block = received.shape[1], table.shape[-1]
    vmem = pl.BlockSpec(memory_space=pltpu.VMEM)
    return pl.pallas_call(
        gathered_kernel,
        out_shape=[jax.ShapeDtypeStruct((rows, block), F32)] * 2,
        in_specs=[vmem, pl.BlockSpec(memory_space=pl.ANY)],
        out_specs=[vmem, vmem],
        scratch_shapes=[pltpu.VMEM(table.shape[1:], BF16), pltpu.SemaphoreType.DMA],
        compiler_params=pltpu.CompilerParams(vmem_limit_bytes=40 * 2**20),
    )(received, table)


def slot_orders(values):
    half = values.shape[1] // 2
    low, high = values[:, :half], values[:, half:]
    back_high = high[:, :0:-1]
    direct = jnp.concatenate([low, high[:, :1], back_high], axis=1)
    mirror = jnp.concatenate([low[:, :1], back_high, high[:, :1], low[:, 1:]], axis=1)
    return jnp.concatenate([direct.reshape(1, -1), mirror.reshape(1, -1)], axis=1)


def plane_weights(dest, eighths, planes, density):
    plane = jnp.arange(planes, dtype=jnp.int32)[:, None]
    shift = plane - dest
    spread = jnp.zeros(shift.shape, BF16)
    for g in range(-2, 4):
        distance = g - eighths.astype(F32) * 0.125
        weight = (jnp.exp(-0.5 * distance * distance) * density).astype(BF16)
        spread = jnp.where(shift == g, weight, spread)
    update = jnp.asarray(update_matrix(planes))
    return jnp.dot(update, spread, preferred_element_type=F32).astype(BF16)


def on_device(projections, dest_plane, sub_offset, ky_bin):
    count_ang = lax.axis_size("ang")
    count_slab = lax.axis_size("slab")
    local_count, quarter, full_width = projections.shape
    height = quarter * count_ang
    planes = Z_DEV * count_slab
    unitary = 1.0 / math.sqrt(height * full_width)
    density = 1.0 / math.sqrt(local_count * count_slab)
    if count_ang == 4 and count_slab == 8:
        mine = fused(
            projections.reshape(local_count * quarter, full_width),
            dest_plane,
            sub_offset,
            ky_bin,
            local_count,
            planes,
            count_slab // 2,
            height,
            unitary,
            density,
        )
        real, imag = gathered_columns(mine, jnp.asarray(placement(full_width, count_ang)))
        return (real.reshape(Z_DEV, KY, -1), imag.reshape(Z_DEV, KY, -1))
    table = jnp.asarray(column_table(full_width, count_ang))
    spectra = column_spectra(projections.reshape(local_count * quarter, full_width), table)
    received = lax.all_to_all(spectra, "ang", split_axis=0, concat_axis=0, tiled=True)
    received = received.reshape(count_ang, local_count, quarter, -1)
    weights = plane_weights(slot_orders(dest_plane), slot_orders(sub_offset), planes, density)
    blocks = gridded_blocks(received, weights, slot_orders(ky_bin), planes, unitary)
    mine = lax.psum_scatter(blocks, "slab", scatter_dimension=0, tiled=True)
    mine = lax.all_to_all(mine.reshape(mine.shape[1:]), "ang", split_axis=0, concat_axis=0, tiled=True)
    real, imag = placed_columns(mine, jnp.asarray(placement(full_width, count_ang)), lax.axis_index("ang"))
    return (real.reshape(Z_DEV, KY, -1), imag.reshape(Z_DEV, KY, -1))


def solution(mesh):
    placed = (P("slab", "ang", None), P("slab", None), P("slab", None), P("slab", None))
    return jax.shard_map(
        on_device,
        mesh=mesh,
        in_specs=placed,
        out_specs=(P("slab", None, "ang"), P("slab", None, "ang")),
        check_vma=False,
    )
```

```python
import functools
import math

import jax
import jax.numpy as jnp
import ml_dtypes
import numpy as np
from jax import lax
from jax.experimental import pallas as pl
from jax.experimental.pallas import tpu as pltpu
from jax.sharding import PartitionSpec as P

Z_DEV = 32
KY = 8
REG_ITERS = 2
SLOPE_LOW, SLOPE_HIGH = 8, 16
CHUNK = 256
BF16 = jnp.bfloat16
MESH = pl.DeviceIdType.MESH
F32 = jnp.float32


def trig_values(length):
    phase = np.arange(length, dtype=np.float32) * np.float32(2.0 * math.pi / length)
    return np.cos(phase), np.sin(phase)


def column_table(width, groups):
    cos, sin = trig_values(width)
    count = width // 2 // groups
    w = np.arange(width)[:, None]
    tables = []
    for j in range(groups):
        phase = w * (groups * np.arange(count) + j)[None, :] % width
        real, imag = cos[phase], -sin[phase]
        if j == 0:
            imag[:, 0] = cos[w[:, 0] * (width // 2) % width]
        tables.append(np.concatenate([real, imag], axis=1))
    return np.stack(tables).astype(ml_dtypes.bfloat16)


def row_tables(height):
    cos, sin = trig_values(height)
    phase = np.arange(height // 2)[:, None] * np.arange(height)[None, :] % height
    cosines, sines = cos[phase], sin[phase]
    sines[0] = cos[np.arange(height) * (height // 2) % height]
    return cosines.astype(ml_dtypes.bfloat16), sines.astype(ml_dtypes.bfloat16)


def update_matrix(planes):
    eye = np.eye(planes)
    lap = 2.0 * eye - np.eye(planes, k=1) - np.eye(planes, k=-1)
    total = eye
    for sweep in range(REG_ITERS):
        total = total - 0.25 * ((total - eye) + lap @ total)
    return total.astype(ml_dtypes.bfloat16)


def placement(width, groups):
    block = width // groups
    half = block // groups
    out = np.zeros((groups, 2, groups * half, block), np.float32)
    for dest in range(groups):
        for j in range(groups):
            for m in range(half):
                if dest < groups // 2:
                    column, sign = groups * m + j, 1.0
                else:
                    column = block - (groups * m + j)
                    column, sign = (0 if j == 0 and m == 0 else column), -1.0
                out[dest, 0, j * half + m, column] = 1.0
                out[dest, 1, j * half + m, column] = sign
    return out.astype(ml_dtypes.bfloat16)


def needs(planes, height, local_count):
    half = height // 2
    per_sign = half // CHUNK
    table = np.zeros((planes // Z_DEV, 2, local_count * 2 * per_sign), np.int32)
    up = np.arange(half)
    down = np.concatenate([[-half], -np.arange(1, half)])
    mirror_up = np.concatenate([[0], -np.arange(1, half)])
    mirror_down = np.concatenate([[-half], np.arange(1, half)])
    for kind, signs in enumerate(((up, down), (mirror_up, mirror_down))):
        for sign, rows in enumerate(signs):
            for part in range(per_sign):
                f = rows[part * CHUNK : (part + 1) * CHUNK].astype(np.int64)
                reach = [(64 * planes * f // (height * s)) // 8 + planes // 2 for s in range(SLOPE_LOW, SLOPE_HIGH + 1)]
                low = np.min(reach, axis=0) - 2 - REG_ITERS
                high = np.max(reach, axis=0) + 3 + REG_ITERS
                for b in range(planes // Z_DEV):
                    hit = np.any((high >= b * Z_DEV) & (low < (b + 1) * Z_DEV))
                    for p in range(local_count):
                        table[b, kind, (p * 2 + sign) * per_sign + part] = int(hit)
    return table.reshape(-1)


def columns_kernel(x_ref, t_ref, o_ref):
    o_ref[0] = jnp.dot(x_ref[...], t_ref[0], preferred_element_type=F32).astype(o_ref.dtype)


def column_spectra(rows, table):
    groups, width, columns = table.shape
    count = rows.shape[0]
    return pl.pallas_call(
        columns_kernel,
        grid=(groups,),
        out_shape=jax.ShapeDtypeStruct((groups, count, columns), BF16),
        in_specs=[
            pl.BlockSpec((count, width), lambda j: (0, 0)),
            pl.BlockSpec((1, width, columns), lambda j: (j, 0, 0)),
        ],
        out_specs=pl.BlockSpec((1, count, columns), lambda j: (j, 0, 0)),
        compiler_params=pltpu.CompilerParams(vmem_limit_bytes=40 * 2**20),
        cost_estimate=pl.CostEstimate(
            flops=2 * count * width * columns * groups, bytes_accessed=12 * 2**20, transcendentals=0
        ),
    )(rows, table)


def grid_kernel(local_count, unitary, need_ref, r_ref, cos_ref, sin_ref, v_ref, ky_ref, o_ref, spec_d, spec_m, acc_d, acc_m):
    step = pl.program_id(0)
    half, height = cos_ref.shape
    columns = r_ref.shape[-1]
    quarter = columns // 4
    chunks = local_count * height // CHUNK

    @pl.when(step < local_count)
    def _():
        rows = r_ref[...].reshape(height, columns)
        cosine = jnp.dot(cos_ref[...], rows, preferred_element_type=F32)
        sine = jnp.dot(sin_ref[...], rows, preferred_element_type=F32)
        first = lax.broadcasted_iota(jnp.int32, (half, columns), 0) == 0
        other = jnp.where(first, sine, cosine)
        sine = jnp.where(first, 0.0, sine)
        lane = lax.broadcasted_iota(jnp.int32, (half, quarter), 1)
        packed = jnp.logical_and(lane == 0, lax.axis_index("ang") == 0)

        def part(a, i):
            return a[:, i * quarter : (i + 1) * quarter]

        for sign, (c, s) in enumerate(((cosine, sine), (other, -sine))):
            re0 = part(c, 0) + jnp.where(packed, 0.0, part(s, 2))
            im0 = jnp.where(packed, 0.0, part(c, 2)) - part(s, 0)
            re1 = part(c, 1) + part(s, 3)
            im1 = part(c, 3) - part(s, 1)
            re0m = jnp.where(packed, jnp.broadcast_to(re1[:, :1], re0.shape), re0)
            im0m = jnp.where(packed, jnp.broadcast_to(im1[:, :1], im0.shape), im0)
            re1m = jnp.where(packed, part(c, 2), re1)
            im1m = jnp.where(packed, -part(s, 2), im1)
            base = pl.multiple_of((step * 2 + sign) * half, half)
            for i, value in enumerate((re0, im0, re1, im1)):
                spec_d[pl.ds(base, half), i * quarter : (i + 1) * quarter] = (value * unitary).astype(BF16)
            for i, value in enumerate((re1m, im1m, re0m, im0m)):
                spec_m[pl.ds(base, half), i * quarter : (i + 1) * quarter] = (value * unitary).astype(BF16)

    @pl.when(step >= local_count)
    def _():
        block = step - local_count
        acc_d[...] = jnp.zeros_like(acc_d)
        acc_m[...] = jnp.zeros_like(acc_m)
        ky_row = lax.broadcasted_iota(jnp.int32, (KY, CHUNK), 0)
        for kind, (spec, acc) in enumerate(((spec_d, acc_d), (spec_m, acc_m))):
            for c in range(chunks):

                @pl.when(need_ref[(block * 2 + kind) * chunks + c] != 0)
                def _(kind=kind, spec=spec, acc=acc, c=c):
                    at = kind * chunks * CHUNK + c * CHUNK
                    weight = v_ref[:, at : at + CHUNK].astype(F32)
                    hit = ky_ref[:, at : at + CHUNK] == ky_row
                    spread = jnp.where(hit[None], weight[:, None, :], 0.0)
                    spread = spread.reshape(Z_DEV * KY, CHUNK).astype(BF16)
                    acc[...] += jnp.dot(spread, spec[c * CHUNK : (c + 1) * CHUNK, :], preferred_element_type=F32)

        for i, acc in enumerate((acc_d, acc_m)):
            for h in range(2):
                o_ref[0, i * 2 + h] = acc[:, h * 2 * quarter : (h + 1) * 2 * quarter].astype(BF16)


def gridded_blocks(received, weights, ky, planes, unitary):
    groups, local_count, quarter_rows, columns = received.shape
    height = groups * quarter_rows
    cosines, sines = row_tables(height)
    blocks = planes // Z_DEV
    chunk_count = local_count * height
    block_of = lambda i, need: (jnp.maximum(i - local_count, 0), 0)
    whole = lambda i, need: (0, 0)
    return pl.pallas_call(
        functools.partial(grid_kernel, local_count, unitary),
        out_shape=jax.ShapeDtypeStruct((blocks, 4, Z_DEV * KY, columns // 2), BF16),
        grid_spec=pltpu.PrefetchScalarGridSpec(
            num_scalar_prefetch=1,
            grid=(local_count + blocks,),
            in_specs=[
                pl.BlockSpec(
                    (groups, 1, quarter_rows, columns),
                    lambda i, need: (0, jnp.minimum(i, local_count - 1), 0, 0),
                ),
                pl.BlockSpec(cosines.shape, whole),
                pl.BlockSpec(sines.shape, whole),
                pl.BlockSpec((Z_DEV, 2 * chunk_count), block_of),
                pl.BlockSpec((1, 2 * chunk_count), whole),
            ],
            out_specs=pl.BlockSpec(
                (1, 4, Z_DEV * KY, columns // 2),
                lambda i, need: (jnp.maximum(i - local_count, 0), 0, 0, 0),
            ),
            scratch_shapes=[
                pltpu.VMEM((chunk_count, columns), BF16),
                pltpu.VMEM((chunk_count, columns), BF16),
                pltpu.VMEM((Z_DEV * KY, columns), F32),
                pltpu.VMEM((Z_DEV * KY, columns), F32),
            ],
        ),
        compiler_params=pltpu.CompilerParams(vmem_limit_bytes=48 * 2**20),
        cost_estimate=pl.CostEstimate(
            flops=2 * chunk_count * height * columns + 2 * blocks * Z_DEV * KY * chunk_count * columns,
            bytes_accessed=12 * 2**20,
            transcendentals=0,
        ),
    )(jnp.asarray(needs(planes, height, local_count)), received, jnp.asarray(cosines), jnp.asarray(sines), weights, ky)


def place_kernel(x_ref, p_ref, real_ref, imag_ref):
    groups, rows, columns = x_ref.shape
    half = columns // 2
    for i, out in enumerate((real_ref, imag_ref)):
        total = None
        for j in range(groups):
            term = jnp.dot(
                x_ref[j, :, i * half : (i + 1) * half],
                p_ref[0, i, j * half : (j + 1) * half, :],
                preferred_element_type=F32,
            )
            total = term if total is None else total + term
        out[...] = total


def placed_columns(received, table, me):
    groups, rows, columns = received.shape
    block = table.shape[-1]
    return pl.pallas_call(
        place_kernel,
        out_shape=[jax.ShapeDtypeStruct((rows, block), F32)] * 2,
        compiler_params=pltpu.CompilerParams(vmem_limit_bytes=40 * 2**20),
    )(received, lax.dynamic_slice_in_dim(table, me, 1, 0))


def fused_kernel(
    sizes,
    x_ref,
    table_ref,
    cos_ref,
    sin_ref,
    update_ref,
    dest_ref,
    eighth_ref,
    ky_ref,
    out_ref,
    table,
    index_ref,
    send_a,
    recv_a,
    weights,
    acc_c,
    acc_s,
    spec_d,
    spec_m,
    spread,
    pair_out,
    pair_in,
    total,
    from_low,
    from_high,
    own,
    got,
    table_sem,
    a_send,
    a_recv,
    pair_send,
    pair_recv,
    line_send,
    low_recv,
    high_recv,
    f_send,
    f_recv,
):
    local_count, planes, chips, unitary, density = sizes
    me = lax.axis_index("ang")
    slab = lax.axis_index("slab")
    z = slab // 2
    core = slab % 2
    half, height = cos_ref.shape
    quarter_rows = height // 4
    columns = recv_a.shape[-1]
    quarter = columns // 4
    chunks = height // CHUNK
    peers = (3 - me, (me + 2) % 4, me + 1 - 2 * (me % 2), me)
    other_core = slab + 1 - 2 * core

    def table_copy(t):
        return pltpu.make_async_copy(table_ref.at[peers[t]], table.at[t], table_sem.at[t])

    for t in range(4):
        table_copy(t).start()

    barrier = pltpu.get_barrier_semaphore()
    for t in range(3):
        pl.semaphore_signal(barrier, inc=1, device_id={"ang": peers[t]}, device_id_type=MESH)
    pl.semaphore_signal(barrier, inc=1, device_id={"slab": other_core}, device_id_type=MESH)

    @pl.when(z > 0)
    def _():
        pl.semaphore_signal(barrier, inc=1, device_id={"slab": slab - 2}, device_id_type=MESH)

    @pl.when(z < chips - 1)
    def _():
        pl.semaphore_signal(barrier, inc=1, device_id={"slab": slab + 2}, device_id_type=MESH)

    at_end = jnp.logical_or(z == 0, z == chips - 1)

    @pl.when(at_end)
    def _():
        pl.semaphore_wait(barrier, 5)

    @pl.when(jnp.logical_not(at_end))
    def _():
        pl.semaphore_wait(barrier, 6)

    def a_copy(t):
        return pltpu.make_async_remote_copy(
            src_ref=send_a.at[t],
            dst_ref=recv_a.at[t],
            send_sem=a_send.at[t],
            recv_sem=a_recv.at[t],
            device_id={"ang": peers[t]},
            device_id_type=MESH,
        )

    for t in range(4):
        table_copy(t).wait()
        target = send_a if t < 3 else recv_a
        target[t] = jnp.dot(x_ref[...], table[t], preferred_element_type=F32).astype(BF16)
        if t < 3:
            a_copy(t).start()

    held = 8
    raw = jnp.concatenate([dest_ref[...], eighth_ref[...], ky_ref[...]], axis=0)
    raw = jnp.concatenate([raw, jnp.zeros((held - raw.shape[0], height), jnp.int32)], axis=0)
    low, high = raw[:, :half], raw[:, half:]
    row = lax.broadcasted_iota(jnp.int32, (half, half), 0)
    flip = (row + lax.broadcasted_iota(jnp.int32, (half, half), 1) == half).astype(F32).astype(BF16)
    back = jnp.dot(high.astype(F32).astype(BF16), flip, preferred_element_type=F32).astype(jnp.int32)
    lane_0 = lax.broadcasted_iota(jnp.int32, (held, half), 1) == 0
    low_0 = jnp.broadcast_to(low[:, :1], low.shape)
    high_0 = jnp.broadcast_to(high[:, :1], high.shape)
    orders = (
        low,
        jnp.where(lane_0, high_0, back),
        jnp.where(lane_0, low_0, back),
        jnp.where(lane_0, high_0, low),
    )
    for kind in range(2):
        for p in range(local_count):
            for sign in range(2):
                at = ((kind * local_count + p) * 2 + sign) * half
                for i in range(3):
                    source = i * local_count + p
                    index_ref[i : i + 1, at : at + half] = orders[kind * 2 + sign][source : source + 1, :]

    def weigh(i, carry):
        at = pl.ds(pl.multiple_of(i * CHUNK, CHUNK), CHUNK)
        shift = lax.broadcasted_iota(jnp.int32, (planes, CHUNK), 0) - index_ref[0:1, at]
        eighth = index_ref[1:2, at].astype(F32) * 0.125
        window = jnp.zeros((planes, CHUNK), F32)
        for g in range(-2, 4):
            distance = g - eighth
            weight = jnp.exp(-0.5 * distance * distance) * density
            window = jnp.where(shift == g, weight, window)
        value = jnp.dot(update_ref[...], window.astype(BF16), preferred_element_type=F32)
        weights[...] = value
        hit = index_ref[2:3, at] == lax.broadcasted_iota(jnp.int32, (KY, CHUNK), 0)

        def scatter(block, inner):
            plane = pl.ds(pl.multiple_of(block * Z_DEV, Z_DEV), Z_DEV)
            cells = jnp.where(hit[None], weights[plane, :][:, None, :], 0.0)
            spread[block, :, at] = cells.reshape(Z_DEV * KY, CHUNK).astype(BF16)
            return inner

        lax.fori_loop(0, planes // Z_DEV, scatter, 0)
        return carry

    lax.fori_loop(0, 2 * local_count * chunks, weigh, 0)

    for t in (3, 2, 1, 0):
        if t < 3:
            a_copy(t).wait()
        at = pl.ds(pl.multiple_of(peers[t] * quarter_rows, quarter_rows), quarter_rows)
        for p in range(local_count):
            rows = recv_a[t, p * quarter_rows : (p + 1) * quarter_rows, :]
            for trig, acc in ((cos_ref, acc_c), (sin_ref, acc_s)):
                term = jnp.dot(trig[:, at], rows, preferred_element_type=F32)
                acc[p] = term if t == 3 else acc[p] + term

    def finish(p, carry):
        cosine, sine = acc_c[p], acc_s[p]
        first = lax.broadcasted_iota(jnp.int32, (half, columns), 0) == 0
        other = jnp.where(first, sine, cosine)
        sine = jnp.where(first, 0.0, sine)
        lane = lax.broadcasted_iota(jnp.int32, (half, quarter), 1)
        packed = jnp.logical_and(lane == 0, me == 0)

        def part(a, i):
            return a[:, i * quarter : (i + 1) * quarter]

        for sign, (c, s) in enumerate(((cosine, sine), (other, -sine))):
            re0 = part(c, 0) + jnp.where(packed, 0.0, part(s, 2))
            im0 = jnp.where(packed, 0.0, part(c, 2)) - part(s, 0)
            re1 = part(c, 1) + part(s, 3)
            im1 = part(c, 3) - part(s, 1)
            re0m = jnp.where(packed, re1, re0)
            im0m = jnp.where(packed, im1, im0)
            re1m = jnp.where(packed, part(c, 2), re1)
            im1m = jnp.where(packed, -part(s, 2), im1)
            at = pl.ds(pl.multiple_of((p * 2 + sign) * half, half), half)
            for i, value in enumerate((re0, im0, re1, im1)):
                spec_d[at, i * quarter : (i + 1) * quarter] = (value * unitary).astype(BF16)
            for i, value in enumerate((re1m, im1m, re0m, im0m)):
                spec_m[at, i * quarter : (i + 1) * quarter] = (value * unitary).astype(BF16)
        return carry

    lax.fori_loop(0, local_count, finish, 0)

    slots = local_count * height

    def piece(block, i):
        kind, side = i // 2, i % 2
        spec = (spec_d, spec_m)[kind]
        return jnp.dot(
            spread[block, :, kind * slots : (kind + 1) * slots],
            spec[:, side * 2 * quarter : (side + 1) * 2 * quarter],
            preferred_element_type=F32,
        )

    def order(t):
        middle = jnp.where(t > 0, (t + 1) % 3 + 1, 0)
        base = jnp.where(jnp.logical_or(z == 0, z == chips - 1), t, middle)
        return jnp.where(z >= chips // 2, base, chips - 1 - base)

    def pair_copy(t):
        return pltpu.make_async_remote_copy(
            src_ref=pair_out.at[t],
            dst_ref=pair_in.at[t],
            send_sem=pair_send.at[t],
            recv_sem=pair_recv.at[t],
            device_id={"slab": other_core},
            device_id_type=MESH,
        )

    def line_copy(t, owner, up, i):
        buffer, sem = (from_low, low_recv) if up else (from_high, high_recv)
        return pltpu.make_async_remote_copy(
            src_ref=total.at[t, i],
            dst_ref=buffer.at[owner, i],
            send_sem=line_send.at[t, i],
            recv_sem=sem.at[owner, i],
            device_id={"slab": slab + 2 if up else slab - 2},
            device_id_type=MESH,
        )

    def add(t, buffer, owner, i):
        total[t, i] = (total[t, i].astype(F32) + buffer[owner, i].astype(F32)).astype(BF16)

    def forward(t):
        owner = order(t)

        @pl.when(owner > z)
        def _():
            for i in peers:

                @pl.when(z > 0)
                def _():
                    line_copy(t, owner, True, i).wait_recv()
                    add(t, from_low, owner, i)

                line_copy(t, owner, True, i).start()

        @pl.when(owner < z)
        def _():
            for i in peers:

                @pl.when(z < chips - 1)
                def _():
                    line_copy(t, owner, False, i).wait_recv()
                    add(t, from_high, owner, i)

                line_copy(t, owner, False, i).start()

    def step(t, carry):
        owner = order(t)
        for i in range(4):
            pair_out[t, i] = piece(owner * 2 + 1 - core, i).astype(BF16)
        pair_copy(t).start()
        for i in range(4):
            own[i] = piece(owner * 2 + core, i)
        pair_copy(t).wait_recv()
        for i in range(4):
            total[t, i] = (own[i] + pair_in[t, i].astype(F32)).astype(BF16)

        @pl.when(jnp.logical_and(at_end, t < chips - 1))
        def _():
            forward(t)

        @pl.when(jnp.logical_and(jnp.logical_not(at_end), t > 0))
        def _():
            forward(t - 1)

        return carry

    lax.fori_loop(0, chips, step, 0)

    last = chips - 1

    def f_copy(t):
        return pltpu.make_async_remote_copy(
            src_ref=total.at[last, peers[t]],
            dst_ref=got.at[t],
            send_sem=f_send.at[t],
            recv_sem=f_recv.at[t],
            device_id={"ang": peers[t]},
            device_id_type=MESH,
        )

    for t in range(4):
        i = peers[t]

        @pl.when(z > 0)
        def _():
            line_copy(last, z, True, i).wait_recv()
            add(last, from_low, z, i)

        @pl.when(z < chips - 1)
        def _():
            line_copy(last, z, False, i).wait_recv()
            add(last, from_high, z, i)

        if t < 3:
            f_copy(t).start()
    out_ref[3] = total[last, me]
    for t in range(3):
        f_copy(t).wait()
        out_ref[t] = got[t]

    def drain(t, carry):
        pair_copy(t).wait_send()

        @pl.when(t < last)
        def _():
            for i in range(4):
                line_copy(t, 0, True, i).wait_send()

        return carry

    lax.fori_loop(0, chips, drain, 0)


def fused(rows, dest, eighths, ky, local_count, planes, chips, height, unitary, density):
    count, width = rows.shape
    table = jnp.asarray(column_table(width, 4))
    columns = table.shape[-1]
    cosines, sines = row_tables(height)
    block = (4, Z_DEV * KY, columns // 2)
    slots = local_count * height
    vmem = pl.BlockSpec(memory_space=pltpu.VMEM)
    anywhere = pl.BlockSpec(memory_space=pl.ANY)
    dma = pltpu.SemaphoreType.DMA
    return pl.pallas_call(
        functools.partial(fused_kernel, (local_count, planes, chips, unitary, density)),
        out_shape=jax.ShapeDtypeStruct(block, BF16),
        in_specs=[vmem, anywhere, vmem, vmem, vmem, vmem, vmem, vmem],
        out_specs=vmem,
        scratch_shapes=[
            pltpu.VMEM(table.shape, BF16),
            pltpu.VMEM((8, 2 * slots), jnp.int32),
            pltpu.VMEM((3, count, columns), BF16),
            pltpu.VMEM((4, count, columns), BF16),
            pltpu.VMEM((planes, CHUNK), F32),
            pltpu.VMEM((local_count, height // 2, columns), F32),
            pltpu.VMEM((local_count, height // 2, columns), F32),
            pltpu.VMEM((slots, columns), BF16),
            pltpu.VMEM((slots, columns), BF16),
            pltpu.VMEM((planes // Z_DEV, Z_DEV * KY, 2 * slots), BF16),
            pltpu.VMEM((chips,) + block, BF16),
            pltpu.VMEM((chips,) + block, BF16),
            pltpu.VMEM((chips,) + block, BF16),
            pltpu.VMEM((chips,) + block, BF16),
            pltpu.VMEM((chips,) + block, BF16),
            pltpu.VMEM(block, F32),
            pltpu.VMEM((3,) + block[1:], BF16),
            dma((4,)),
            dma((3,)),
            dma((3,)),
            dma((chips,)),
            dma((chips,)),
            dma((chips, 4)),
            dma((chips, 4)),
            dma((chips, 4)),
            dma((3,)),
            dma((3,)),
        ],
        compiler_params=pltpu.CompilerParams(
            collective_id=0, has_side_effects=True, vmem_limit_bytes=58 * 2**20
        ),
        cost_estimate=pl.CostEstimate(flops=14 * 10**9, bytes_accessed=20 * 2**20, transcendentals=0),
    )(
        rows,
        table,
        jnp.asarray(cosines),
        jnp.asarray(sines),
        jnp.asarray(update_matrix(planes)),
        dest,
        eighths,
        ky,
    )


def gathered_kernel(x_ref, place_ref, real_ref, imag_ref, place, sem):
    me = lax.axis_index("ang")
    copy = pltpu.make_async_copy(place_ref.at[me], place, sem)
    copy.start()
    peers = (3 - me, (me + 2) % 4, me + 1 - 2 * (me % 2), me)
    half = x_ref.shape[-1] // 2
    copy.wait()
    for i, out in enumerate((real_ref, imag_ref)):
        total = None
        for t in range(4):
            at = pl.ds(pl.multiple_of(peers[t] * half, half), half)
            term = jnp.dot(x_ref[t, :, i * half : (i + 1) * half], place[i, at, :], preferred_element_type=F32)
            total = term if total is None else total + term
        out[...] = total


def gathered_columns(received, table):
    rows, block = received.shape[1], table.shape[-1]
    vmem = pl.BlockSpec(memory_space=pltpu.VMEM)
    return pl.pallas_call(
        gathered_kernel,
        out_shape=[jax.ShapeDtypeStruct((rows, block), F32)] * 2,
        in_specs=[vmem, pl.BlockSpec(memory_space=pl.ANY)],
        out_specs=[vmem, vmem],
        scratch_shapes=[pltpu.VMEM(table.shape[1:], BF16), pltpu.SemaphoreType.DMA],
        compiler_params=pltpu.CompilerParams(vmem_limit_bytes=40 * 2**20),
    )(received, table)


def slot_orders(values):
    half = values.shape[1] // 2
    low, high = values[:, :half], values[:, half:]
    back_high = high[:, :0:-1]
    direct = jnp.concatenate([low, high[:, :1], back_high], axis=1)
    mirror = jnp.concatenate([low[:, :1], back_high, high[:, :1], low[:, 1:]], axis=1)
    return jnp.concatenate([direct.reshape(1, -1), mirror.reshape(1, -1)], axis=1)


def plane_weights(dest, eighths, planes, density):
    plane = jnp.arange(planes, dtype=jnp.int32)[:, None]
    shift = plane - dest
    spread = jnp.zeros(shift.shape, BF16)
    for g in range(-2, 4):
        distance = g - eighths.astype(F32) * 0.125
        weight = (jnp.exp(-0.5 * distance * distance) * density).astype(BF16)
        spread = jnp.where(shift == g, weight, spread)
    update = jnp.asarray(update_matrix(planes))
    return jnp.dot(update, spread, preferred_element_type=F32).astype(BF16)


def on_device(projections, dest_plane, sub_offset, ky_bin):
    count_ang = lax.axis_size("ang")
    count_slab = lax.axis_size("slab")
    local_count, quarter, full_width = projections.shape
    height = quarter * count_ang
    planes = Z_DEV * count_slab
    unitary = 1.0 / math.sqrt(height * full_width)
    density = 1.0 / math.sqrt(local_count * count_slab)
    if count_ang == 4 and count_slab == 8:
        mine = fused(
            projections.reshape(local_count * quarter, full_width),
            dest_plane,
            sub_offset,
            ky_bin,
            local_count,
            planes,
            count_slab // 2,
            height,
            unitary,
            density,
        )
        real, imag = gathered_columns(mine, jnp.asarray(placement(full_width, count_ang)))
        return (real.reshape(Z_DEV, KY, -1), imag.reshape(Z_DEV, KY, -1))
    table = jnp.asarray(column_table(full_width, count_ang))
    spectra = column_spectra(projections.reshape(local_count * quarter, full_width), table)
    received = lax.all_to_all(spectra, "ang", split_axis=0, concat_axis=0, tiled=True)
    received = received.reshape(count_ang, local_count, quarter, -1)
    weights = plane_weights(slot_orders(dest_plane), slot_orders(sub_offset), planes, density)
    blocks = gridded_blocks(received, weights, slot_orders(ky_bin), planes, unitary)
    mine = lax.psum_scatter(blocks, "slab", scatter_dimension=0, tiled=True)
    mine = lax.all_to_all(mine.reshape(mine.shape[1:]), "ang", split_axis=0, concat_axis=0, tiled=True)
    real, imag = placed_columns(mine, jnp.asarray(placement(full_width, count_ang)), lax.axis_index("ang"))
    return (real.reshape(Z_DEV, KY, -1), imag.reshape(Z_DEV, KY, -1))


def solution(mesh):
    placed = (P("slab", "ang", None), P("slab", None), P("slab", None), P("slab", None))
    return jax.shard_map(
        on_device,
        mesh=mesh,
        in_specs=placed,
        out_specs=(P("slab", None, "ang"), P("slab", None, "ang")),
        check_vma=False,
    )
```
